32 devices in a mesh: grp: 1, frame: 32 (over z, y, x, core).
Axes of the slice: x: 2, y: 2, z: 4, core: 2. Of those that a mesh axis runs over, the one named last changes fastest.
Arguments:
- tokens: bfloat16 [8192, 2240], P(('grp', 'frame')), may hold values from -16 to 16
- w_query: bfloat16 [1792, 2240], P('frame'), may hold values from -0.125 to 0.125
- w_keyval: bfloat16 [3584, 2240], P('frame'), may hold values from -0.125 to 0.125
- taps: float32 [3, 1792], replicated, may hold values from -1 to 1
Outputs:
- mixed: bfloat16 [8192, 1792], P(('grp', 'frame'))
The draws below stay inside these ranges and needn't reach their ends.
All inputs are finite; a program needn't handle non-finite values.
Results may differ from the reference program's by a relative error of at most 0.0051.
Values may be sent and summed in bfloat16 or wider, within the bound.
No kernel may reach another device: no remote copies, remote signals or barrier semaphores. Data moves between devices by JAX's collectives and lax.ppermute only.
A program may use at most 128 MiB of HBM per device.

```python
import jax
import jax.numpy as jnp
from jax import lax

D = 2240
HEADS = 16
HDIM = 112
HEIGHT = 32
WIDTH = 32
TOK_DEV = 256
FRAMES = 8
TOKENS = 8192
CH = 1792


def draw_tokens(key, part):
    key_noise, key_level, key_offset = jax.random.split(key, 3)
    blocks = TOKENS // TOK_DEV
    rising = 3.0 ** (jnp.arange(blocks, dtype=jnp.float32) / max(blocks - 1, 1))
    level = jax.random.uniform(key_level, (blocks, 1), jnp.float32, 0.7, 1.4) * rising[:, None]
    offsets = jax.random.normal(key_offset, (blocks, D), jnp.float32) * level
    noise = jax.random.normal(key_noise, (TOKENS, D), jnp.float32)
    values = noise + jnp.repeat(offsets, TOK_DEV, axis=0)
    return jnp.clip(values, -16.0, 16.0).astype(jnp.bfloat16)


def levels(rng, shape, cuts, smallest, high):
    gain = 1.0
    for axis_at, shards_of in cuts:
        heights = jax.random.uniform(jax.random.fold_in(jax.random.fold_in(rng, 6), axis_at), (shards_of,), jnp.float32, smallest / len(cuts), high / len(cuts))
        gain = gain * jnp.repeat(jnp.exp(heights), shape[axis_at] // shards_of).reshape((-1,) + (1,) * (len(shape) - 1 - axis_at))
    return gain


def scatter_about(own_key, dims, spread, bound, pieces=(), held_as=jnp.bfloat16):
    values = jax.random.normal(own_key, dims, jnp.float32) * spread
    if len(pieces) > 0:
        values = levels(own_key, dims, pieces, -0.22, 0.18) * values
    return jnp.clip(values, min=-bound, max=bound).astype(held_as)


def setup_inputs(seed: int = 0, part: int = 0) -> dict:
    keys = jax.random.split(jax.random.key(seed), 5)
    part_keys = jax.random.split(jax.random.fold_in(keys[4], part), 5)
    return {
        "tokens": draw_tokens(jax.random.fold_in(jax.random.fold_in(keys[4], part), 71), part),
        "w_query": scatter_about(keys[1], (CH, D), D ** -0.5, 0.125, ((0, 32),)),
        "w_keyval": scatter_about(keys[2], (2 * CH, D), D ** -0.5, 0.125, ((0, 32),)),
        "taps": jnp.clip(jax.random.uniform(keys[3], (3, CH), jnp.float32, -1.0, 1.0), -1.0, 1.0),
    }


epsilon = 1e-06

def normalize(rows_in):
    values = rows_in.astype(jnp.float32)
    scale_inv = lax.rsqrt(lax.optimization_barrier(jnp.mean(values * values, axis=-1, keepdims=True)) + epsilon)
    return (values * scale_inv).astype(jnp.bfloat16)

def temporal_mix(by_frame, taps):
    zeros_row = jnp.zeros_like(by_frame[:1])
    earlier = jnp.concatenate([zeros_row, by_frame[:-1]], 0)
    later_frame = jnp.concatenate([by_frame[1:], zeros_row], 0)
    return taps[0] * earlier + taps[1] * by_frame + taps[2] * later_frame

def reference(tokens, w_query, w_keyval, taps):
    channels = HEADS * HDIM
    blocks = TOKENS // TOK_DEV

    def project(block_rows):
        normed = normalize(block_rows)
        query_lin = jnp.dot(normed, w_query.T, preferred_element_type=jnp.float32)
        keyval_lin = jnp.dot(normed, w_keyval.T, preferred_element_type=jnp.float32)
        query_feats = jax.nn.relu(query_lin).astype(jnp.bfloat16)
        key_feats = jax.nn.relu(keyval_lin[:, :channels]).astype(jnp.bfloat16)
        value_proj = keyval_lin[:, channels:].astype(jnp.bfloat16)
        key_heads = key_feats.astype(jnp.float32).reshape(-1, HEADS, HDIM)
        value_heads = value_proj.astype(jnp.float32).reshape(-1, HEADS, HDIM)
        state = jnp.einsum('thd,the->hde', key_heads, value_heads, precision=lax.Precision.HIGHEST)
        return (query_feats, state, lax.optimization_barrier(jnp.sum(key_heads, axis=0)))
    query_feats, states, key_sums = lax.map(project, tokens.reshape(blocks, TOK_DEV, D))
    state = lax.optimization_barrier(jnp.sum(states, axis=0))
    key_total = lax.optimization_barrier(jnp.sum(key_sums, axis=0))
    query_heads = query_feats.reshape(TOKENS, HEADS, HDIM).astype(jnp.float32)
    numer = jnp.einsum('thd,hde->the', query_heads, state, precision=lax.Precision.HIGHEST)
    denom = jnp.einsum('thd,hd->th', query_heads, key_total, precision=lax.Precision.HIGHEST) + epsilon
    attended = (numer / denom[:, :, None]).reshape(TOKENS, channels).astype(jnp.bfloat16)
    by_frame = attended.reshape(FRAMES, HEIGHT * WIDTH, channels).astype(jnp.float32)
    return temporal_mix(by_frame, taps).reshape(TOKENS, channels).astype(jnp.bfloat16)
```

```python
import jax
import jax.numpy as jnp
from jax import lax
from jax.sharding import PartitionSpec as P

HEADS = 16
HDIM = 112
HEIGHT = 32
WIDTH = 32


epsilon = 1e-06


def from_behind(value, axis, steps):
    count = lax.axis_size(axis)
    leading, last = (max(0, -steps), min(count, count - steps))
    return lax.ppermute(value, axis, [(source, source + steps) for source in range(leading, last)])


def normalize(rows_in):
    values = rows_in.astype(jnp.float32)
    scale_inv = lax.rsqrt(jnp.mean(values * values, axis=-1, keepdims=True) + epsilon)
    return (values * scale_inv).astype(jnp.bfloat16)


def project(rows, weight_rows):
    return lax.dot_general(
        rows, weight_rows, (((1,), (1,)), ((), ())), preferred_element_type=jnp.float32
    )


def gathered(tokens, w_query, w_keyval, taps):
    channels = HEADS * HDIM
    rows_here = tokens.shape[0]
    normed = normalize(tokens)
    keyval_lin = project(normed, lax.all_gather(w_keyval, "frame", axis=0, tiled=True))
    key_feats = jax.nn.relu(keyval_lin[:, :channels]).astype(jnp.bfloat16)
    value_proj = keyval_lin[:, channels:].astype(jnp.bfloat16)
    key_heads = key_feats.reshape(rows_here, HEADS, HDIM)
    value_heads = value_proj.reshape(rows_here, HEADS, HDIM)
    local_state = jnp.einsum(
        "thd,the->hde", key_heads, value_heads, preferred_element_type=jnp.float32
    )
    local_keys = jnp.sum(key_heads.astype(jnp.float32), axis=0)
    query_lin = project(normed, lax.all_gather(w_query, "frame", axis=0, tiled=True))
    query_feats = jax.nn.relu(query_lin).astype(jnp.bfloat16)
    state, key_total = lax.psum((local_state, local_keys), "frame")
    query_heads = query_feats.reshape(rows_here, HEADS, HDIM).astype(jnp.float32)
    numer = jnp.einsum("thd,hde->the", query_heads, state, precision=lax.Precision.HIGHEST)
    denom = (
        jnp.einsum("thd,hd->th", query_heads, key_total, precision=lax.Precision.HIGHEST) + epsilon
    )
    attended = (numer / denom[:, :, None]).reshape(rows_here, channels).astype(jnp.bfloat16)
    strips = HEIGHT * WIDTH // rows_here
    earlier = from_behind(attended, "frame", strips)
    later_frame = from_behind(attended, "frame", -strips)
    mixed = (
        taps[0] * earlier.astype(jnp.float32)
        + taps[1] * attended.astype(jnp.float32)
        + taps[2] * later_frame.astype(jnp.float32)
    ).astype(jnp.bfloat16)
    return mixed


LAYERS = 4
PLANE = 8


def send(value, place):
    pairs = []
    for z in range(LAYERS):
        for slot in range(PLANE):
            to = place(z, slot)
            if to is not None:
                pairs.append((z * PLANE + slot, to[0] * PLANE + to[1]))
    return lax.ppermute(value, "frame", pairs)


def swap(value, bits):
    return send(value, lambda z, slot: (z, slot ^ bits))


def between(value, steps):
    return send(value, lambda z, slot: (steps[z], slot) if z in steps else None)


def pick(flag, first, second):
    return jnp.where(flag, first, second)


def attend(query, state):
    high = state.astype(jnp.bfloat16)
    low = (state - high.astype(jnp.float32)).astype(jnp.bfloat16)
    both = jnp.dot(query, high, preferred_element_type=jnp.float32) + jnp.dot(
        query, low, preferred_element_type=jnp.float32
    )
    return (both[:, :HDIM] / (both[:, HDIM:] + epsilon)).astype(jnp.bfloat16)


def planes(tokens, w_query, w_keyval, taps):
    me = lax.axis_index("frame")
    z, slot = me // PLANE, me % PLANE
    y = slot // 4
    rows_here = tokens.shape[0]

    keyval = [w_keyval, None, None, None]
    keyval[2] = between(w_keyval, {0: 2, 2: 0, 1: 3, 3: 1})
    keyval[1] = between(w_keyval, {0: 1, 1: 0, 2: 3, 3: 2})
    inner = between(w_keyval, {1: 2, 2: 1})

    blocks = [None] * PLANE
    blocks[0] = normalize(tokens)
    blocks[2] = swap(blocks[0], 2)
    blocks[4] = swap(blocks[0], 4)
    blocks[1] = swap(blocks[0], 1)

    def home(z, slot, half):
        head = (z * PLANE + slot) // 2
        return (z, head % PLANE) if slot % 2 == half else None

    halves = [send(w_query, lambda z, slot, half=half: home(z, slot, half)) for half in range(2)]
    query_here = jnp.concatenate(halves, axis=0)

    outer = between(keyval[2], {1: 0, 2: 3})
    keyval[3] = inner + outer

    half_rows = rows_here // 2
    low = swap(blocks[2][:half_rows], 4)
    high = swap(blocks[4][half_rows:], 2)
    blocks[3] = swap(blocks[2], 1)
    blocks[5] = swap(blocks[4], 1)

    def query_out(z, slot):
        return (z ^ 1, slot) if z % 2 == slot // 4 else None

    query_near = query_here + send(query_here, query_out)
    query_inner = between(query_near, {1: 2, 2: 1})
    query_far = query_inner + between(query_inner, {1: 0, 2: 3})

    blocks[6] = jnp.concatenate([low, high], axis=0)
    blocks[7] = jnp.concatenate([swap(low, 1), swap(high, 1)], axis=0)

    ones = jnp.ones((2 * rows_here, 1), jnp.bfloat16)
    partial = [0.0, 0.0]
    chunks = [
        jnp.concatenate([blocks[k], blocks[k + 1]], axis=0) for k in range(0, PLANE, 2)
    ]
    keys_first = z < 2
    for chunk in chunks:
        lin = [project(chunk, rows) for rows in keyval]
        for pair in range(2):
            key = jax.nn.relu(pick(keys_first, lin[pair], lin[pair + 2])).astype(jnp.bfloat16)
            value = pick(keys_first, lin[pair + 2], lin[pair]).astype(jnp.bfloat16)
            partial[pair] += lax.dot_general(
                key,
                jnp.concatenate([value, ones], axis=1),
                (((0,), (0,)), ((), ())),
                preferred_element_type=jnp.float32,
            )
    odd = z % 2 == 1
    state = jnp.stack([pick(odd, partial[1], partial[0]), pick(odd, partial[0], partial[1])])
    state = state + between(state, {0: 1, 1: 0, 2: 3, 3: 2})
    state = state + between(state, {0: 2, 2: 0, 1: 3, 3: 1})

    near_first = z < 2
    queries = []
    for rows in (pick(near_first, query_near, query_far), pick(near_first, query_far, query_near)):
        queries.append(
            [jax.nn.relu(project(chunk, rows)).astype(jnp.bfloat16) for chunk in chunks]
        )
    mine = [jnp.concatenate(parts[:2], axis=0) for parts in queries]
    other = [jnp.concatenate(parts[2:], axis=0) for parts in queries]
    even_row = y == 0
    frame_a = jnp.concatenate([pick(even_row, m, o) for m, o in zip(mine, other)], axis=1)
    frame_b = jnp.concatenate([pick(even_row, o, m) for m, o in zip(mine, other)], axis=1)
    before = between(frame_b, {0: 1, 1: 2, 2: 3})
    after = between(frame_a, {1: 0, 2: 1, 3: 2})

    def attended(frame):
        return jnp.concatenate(
            [attend(frame[:, HDIM * i : HDIM * (i + 1)], state[i]) for i in range(2)], axis=1
        ).astype(jnp.float32)

    there_before, there_after = z > 0, z < LAYERS - 1
    att_before = pick(there_before, attended(before), 0.0)
    att_a, att_b = attended(frame_a), attended(frame_b)
    att_after = pick(there_after, attended(after), 0.0)
    by_head = taps.reshape(3, HEADS, HDIM)
    tap = jnp.concatenate(
        [
            lax.dynamic_slice_in_dim(by_head, slot + PLANE * i, 1, axis=1)[:, 0]
            for i in range(2)
        ],
        axis=1,
    )
    mixed_a = (tap[0] * att_before + tap[1] * att_a + tap[2] * att_b).astype(jnp.bfloat16)
    mixed_b = (tap[0] * att_a + tap[1] * att_b + tap[2] * att_after).astype(jnp.bfloat16)
    same = pick(even_row, mixed_a, mixed_b).reshape(2, 2, rows_here, 2 * HDIM)
    cross = pick(even_row, mixed_b, mixed_a).reshape(2, 2, rows_here, 2 * HDIM)
    by_place = jnp.stack([same, cross])
    kept = by_place[:, :, 0]
    given = swap(by_place[:, :, 1], 1)
    odd_core = slot % 2 == 1
    first, second = pick(odd_core, given, kept), pick(odd_core, kept, given)
    whole = jnp.stack(
        [
            jnp.stack([part[..., HDIM * i : HDIM * (i + 1)] for part in (first, second)], axis=3)
            for i in range(2)
        ],
        axis=3,
    ).reshape(2, 2, rows_here, 4 * HDIM)
    got = [
        [whole[0, 0], swap(whole[0, 1], 2)],
        [swap(whole[1, 0], 4), swap(whole[1, 1], 6)],
    ]
    right = (slot // 2) % 2 == 1
    rows = [[pick(right, g[1], g[0]), pick(right, g[0], g[1])] for g in got]
    placed = [pick(even_row, rows[0][i], rows[1][i]) for i in range(2)] + [
        pick(even_row, rows[1][i], rows[0][i]) for i in range(2)
    ]
    out = [part[:, : 2 * HDIM] for part in placed] + [part[:, 2 * HDIM :] for part in placed]
    return jnp.concatenate(out, axis=1)


def local(tokens, w_query, w_keyval, taps):
    fits = (
        lax.axis_size("frame") == LAYERS * PLANE
        and HEADS == 2 * PLANE
        and w_keyval.shape[0] == HDIM
        and 2 * w_query.shape[0] == HDIM
        and PLANE * tokens.shape[0] == 2 * HEIGHT * WIDTH
    )
    return (planes if fits else gathered)(tokens, w_query, w_keyval, taps)


def solution(mesh):
    placed = (P(("grp", "frame"), None), P("frame", None), P("frame", None), P())
    return jax.shard_map(
        local, mesh=mesh, in_specs=placed, out_specs=P(("grp", "frame"), None), check_vma=False
    )
```

```python
import functools

import jax
import jax.numpy as jnp
from jax import lax
from jax.experimental import pallas as pl
from jax.experimental.pallas import tpu as pltpu
from jax.sharding import PartitionSpec as P

HEADS = 16
HDIM = 112
HEIGHT = 32
WIDTH = 32


epsilon = 1e-06


def from_behind(value, axis, steps):
    count = lax.axis_size(axis)
    leading, last = (max(0, -steps), min(count, count - steps))
    return lax.ppermute(value, axis, [(source, source + steps) for source in range(leading, last)])


def normalize(rows_in):
    values = rows_in.astype(jnp.float32)
    scale_inv = lax.rsqrt(jnp.mean(values * values, axis=-1, keepdims=True) + epsilon)
    return (values * scale_inv).astype(jnp.bfloat16)


def gathered(tokens, w_query, w_keyval, taps):
    channels = HEADS * HDIM
    rows_here = tokens.shape[0]
    normed = normalize(tokens)

    def project_rows(weight_rows):
        return lax.dot_general(
            normed, weight_rows, (((1,), (1,)), ((), ())), preferred_element_type=jnp.float32
        )

    keyval_lin = project_rows(lax.all_gather(w_keyval, "frame", axis=0, tiled=True))
    key_feats = jax.nn.relu(keyval_lin[:, :channels]).astype(jnp.bfloat16)
    value_proj = keyval_lin[:, channels:].astype(jnp.bfloat16)
    key_heads = key_feats.reshape(rows_here, HEADS, HDIM)
    value_heads = value_proj.reshape(rows_here, HEADS, HDIM)
    local_state = jnp.einsum(
        "thd,the->hde", key_heads, value_heads, preferred_element_type=jnp.float32
    )
    local_keys = jnp.sum(key_heads.astype(jnp.float32), axis=0)
    query_lin = project_rows(lax.all_gather(w_query, "frame", axis=0, tiled=True))
    query_feats = jax.nn.relu(query_lin).astype(jnp.bfloat16)
    state, key_total = lax.psum((local_state, local_keys), "frame")
    query_heads = query_feats.reshape(rows_here, HEADS, HDIM).astype(jnp.float32)
    numer = jnp.einsum("thd,hde->the", query_heads, state, precision=lax.Precision.HIGHEST)
    denom = (
        jnp.einsum("thd,hd->th", query_heads, key_total, precision=lax.Precision.HIGHEST) + epsilon
    )
    attended = (numer / denom[:, :, None]).reshape(rows_here, channels).astype(jnp.bfloat16)
    strips = HEIGHT * WIDTH // rows_here
    earlier = from_behind(attended, "frame", strips)
    later_frame = from_behind(attended, "frame", -strips)
    mixed = (
        taps[0] * earlier.astype(jnp.float32)
        + taps[1] * attended.astype(jnp.float32)
        + taps[2] * later_frame.astype(jnp.float32)
    ).astype(jnp.bfloat16)
    return mixed


VMEM = pl.BlockSpec(memory_space=pltpu.VMEM)
SMEM = pl.BlockSpec(memory_space=pltpu.SMEM)
PARAMS = pltpu.CompilerParams(vmem_limit_bytes=48 * 2**20)


def kernel_call(body, outs, *operands, scalars=1, scratch=()):
    return pl.pallas_call(
        body,
        out_shape=outs,
        in_specs=[SMEM] * scalars + [VMEM] * (len(operands) - scalars),
        out_specs=jax.tree.map(lambda _: VMEM, outs),
        scratch_shapes=list(scratch),
        compiler_params=PARAMS,
    )(*operands)


def like(shape, dtype=jnp.bfloat16):
    return jax.ShapeDtypeStruct(shape, dtype)


def begin_kernel(tokens, w_query, w_keyval, normed, weights):
    split = w_keyval.shape[0]
    weights[:split] = w_keyval[...]
    weights[split:] = w_query[...]
    depth = tokens.shape[0]
    step = depth // 10
    total = jnp.zeros((1, tokens.shape[1]), jnp.float32)
    for start in range(0, depth, step):
        values = tokens[start : start + step].astype(jnp.float32)
        total += jnp.sum(values * values, axis=0, keepdims=True)
    scale_inv = lax.rsqrt(total / depth + epsilon)
    for start in range(0, depth, step):
        values = tokens[start : start + step].astype(jnp.float32)
        normed[start : start + step] = (values * scale_inv).astype(jnp.bfloat16)


def begin(tokens, w_query, w_keyval):
    rows = w_keyval.shape[0] + w_query.shape[0]
    outs = (like(tokens.shape), like((rows, w_query.shape[1])))
    return kernel_call(begin_kernel, outs, tokens, w_query, w_keyval, scalars=0)


def product(rows, block):
    at, total = 0, None
    for part in block:
        depth = part.shape[0]
        one = jnp.dot(rows[:, at : at + depth], part[...], preferred_element_type=jnp.float32)
        at, total = at + depth, one if total is None else total + one
    return total


def parts_of(refs, shape):
    refs = list(refs)
    return [[refs.pop(0) for _ in block] for block in shape], refs


def state_kernel(pairs, shape, place, *refs):
    rows, refs = parts_of(refs, pairs)
    blocks, (out, held) = parts_of(refs, shape)
    z = place[0]
    for i, row in enumerate(rows):
        to = pl.ds(HDIM * i, HDIM)
        if len(row) == 1:
            held[to] = row[0][:HDIM]
        else:
            middle = (z == 1) | (z == 2)

            @pl.when(middle)
            def _():
                held[to] = row[0][:HDIM]

            @pl.when(jnp.logical_not(middle))
            def _():
                held[to] = row[1][:HDIM]

    keys_first = z < 2
    count = len(rows) // 2
    totals = [0.0] * count
    tokens = blocks[0][0].shape[1]
    ones = (lax.broadcasted_iota(jnp.int32, (16, tokens), 0) == 0).astype(jnp.bfloat16)
    for block in blocks:
        lin = product(held, block)
        for i in range(count):
            one = lin[2 * i * HDIM : (2 * i + 1) * HDIM]
            two = lin[(2 * i + 1) * HDIM : (2 * i + 2) * HDIM]
            key = jnp.maximum(jnp.where(keys_first, one, two), 0.0).astype(jnp.bfloat16)
            value = jnp.where(keys_first, two, one).astype(jnp.bfloat16)
            totals[i] += lax.dot_general(
                jnp.concatenate([value, ones], axis=0),
                key,
                (((1,), (1,)), ((), ())),
                preferred_element_type=jnp.float32,
            )
    for i in range(count):
        out[i] = totals[i]


def states_of(place, rows, blocks):
    depth = rows[0][0].shape[1]
    return kernel_call(
        functools.partial(
            state_kernel, [(0,) * len(row) for row in rows], [(0,) * len(block) for block in blocks]
        ),
        like((len(rows) // 2, HDIM + 16, HDIM), jnp.float32),
        place,
        *[one for row in rows for one in row],
        *[part for block in blocks for part in block],
        scratch=[pltpu.VMEM((len(rows) * HDIM, depth), jnp.bfloat16)],
    )


def query_kernel(shape, place, mine, there, *refs):
    blocks, (frame_a, frame_b) = parts_of(refs, shape)
    y = place[1] // 4
    half = HDIM // 2
    tokens = blocks[0][0].shape[1]
    for k, block in enumerate(blocks):
        one, two = product(mine, block), product(there, block)
        heads = []
        for at in range(0, mine.shape[0], half):
            head = jnp.concatenate([one[at : at + half], two[at : at + half]], axis=0)
            heads.append(jnp.maximum(head, 0.0).astype(jnp.bfloat16))
        feats = jnp.concatenate(heads, axis=0)
        to = slice(tokens * (k % 2), tokens * (k % 2 + 1))

        @pl.when(y == k // 2)
        def _():
            frame_a[:, to] = feats

        @pl.when(y != k // 2)
        def _():
            frame_b[:, to] = feats


def queries_of(place, mine, there, blocks):
    tokens = blocks[0][0].shape[1]
    frame = like((2 * mine.shape[0], 2 * tokens))
    return kernel_call(
        functools.partial(query_kernel, [(0,) * len(block) for block in blocks]),
        (frame, frame),
        place,
        mine,
        there,
        *[part for block in blocks for part in block],
    )


def attend_kernel(place, mine, there, taps, frame_a, frame_b, before, later, *outs):
    z, slot = place[0], place[1]
    y, core = slot // 4, slot % 2
    tokens = outs[0].shape[1]
    half = HDIM // 2
    row = lax.broadcasted_iota(jnp.int32, (HDIM, HDIM), 0)
    column = lax.broadcasted_iota(jnp.int32, (HDIM, HDIM), 1)
    turned = jnp.where(row < half, row + half, row - half)
    order = (column == jnp.where(core == 0, row, turned)).astype(jnp.bfloat16)
    for m in range(LAYERS):
        own, other = mine[m // 2], there[m // 2]
        state = jnp.where(core == m % 2, own, other)
        high = state.astype(jnp.bfloat16)
        low = (state - high.astype(jnp.float32)).astype(jnp.bfloat16)
        both = jnp.concatenate([high, low], axis=0)
        both = jnp.dot(both, order, preferred_element_type=jnp.float32).astype(jnp.bfloat16)
        rows = pl.ds(HDIM * m, HDIM)

        def attended(frame, there=None):
            sums = jnp.dot(both, frame[rows], preferred_element_type=jnp.float32)
            sums = sums[: HDIM + 16] + sums[HDIM + 16 :]
            result = sums[:HDIM] * (1.0 / (sums[HDIM : HDIM + 1] + epsilon))
            result = result.astype(jnp.bfloat16).astype(jnp.float32)
            return result if there is None else jnp.where(there, result, 0.0)

        tap = taps[rows]
        att_before = attended(before, z > 0)
        att_a, att_b = attended(frame_a), attended(frame_b)
        att_later = attended(later, z < LAYERS - 1)
        mixed_a = tap[:, 0:1] * att_before + tap[:, 1:2] * att_a + tap[:, 2:3] * att_b
        mixed_b = tap[:, 0:1] * att_a + tap[:, 1:2] * att_b + tap[:, 2:3] * att_later
        mixed = (jnp.where(y == 0, mixed_a, mixed_b), jnp.where(y == 0, mixed_b, mixed_a))
        for i in range(4):
            at = tokens * (i % 2)
            outs[i][rows] = mixed[i // 2][:, at : at + tokens].astype(jnp.bfloat16)


def attend(place, mine, there, taps, frames):
    channels, tokens = frames[0].shape
    outs = (like((channels, tokens // 2)),) * 4
    return kernel_call(attend_kernel, outs, place, mine, there, taps, *frames)


def finish_kernel(place, *refs):
    parts, (out, held) = refs[:4], refs[4:]
    chip = place[1] // 2
    tokens = out.shape[0]
    for k, part in enumerate(parts):
        for m in range(LAYERS):
            to = pl.multiple_of((4 * m + (chip ^ k)) * HDIM, 16)
            held[pl.ds(to, HDIM)] = part[pl.ds(HDIM * m, HDIM)]
    row = lax.broadcasted_iota(jnp.int32, (tokens, tokens), 0)
    column = lax.broadcasted_iota(jnp.int32, (tokens, tokens), 1)
    same = (row == column).astype(jnp.bfloat16)
    step = 256
    for at in range(0, out.shape[1], step):
        out[:, at : at + step] = lax.dot_general(
            same, held[at : at + step], (((1,), (1,)), ((), ())), preferred_element_type=jnp.float32
        ).astype(jnp.bfloat16)


def finish(place, parts):
    channels, tokens = parts[0].shape
    return kernel_call(
        finish_kernel,
        like((tokens, 4 * channels)),
        place,
        *parts,
        scratch=[pltpu.VMEM((4 * channels, tokens), jnp.bfloat16)],
    )


LAYERS = 4
PLANE = 8


def send(value, place):
    pairs = []
    for z in range(LAYERS):
        for slot in range(PLANE):
            to = place(z, slot)
            if to is not None:
                pairs.append((z * PLANE + slot, to[0] * PLANE + to[1]))
    return lax.ppermute(value, "frame", pairs)


def swap(value, bits):
    return send(value, lambda z, slot: (z, slot ^ bits))


def between(value, steps):
    return send(value, lambda z, slot: (steps[z], slot) if z in steps else None)


def after(value, *others):
    return lax.optimization_barrier((value,) + others)[0]


def planes(tokens, w_query, w_keyval, taps):
    me = lax.axis_index("frame")
    z, slot = me // PLANE, me % PLANE
    chip = slot // 2
    place = jnp.stack([z, slot]).astype(jnp.int32)

    cross = [{i: i ^ k for i in range(LAYERS)} for k in range(LAYERS)]
    inner, outer = {1: 2, 2: 1}, {1: 0, 2: 3}

    blocks = [None] * PLANE
    weights = [None] * LAYERS
    own, weights[0] = begin(tokens.T, w_query, w_keyval)
    weights[2] = between(weights[0], cross[2])
    beside, across = swap(own, 2), swap(own, 4)
    weights[1] = between(weights[0], cross[1])
    own_there = swap(own, 1)
    split = (own.shape[0] // 256) * 128
    low, high = swap(beside[:split], 4), swap(across[split:], 2)
    beside_there = swap(beside, 1)
    weights_inner = between(after(weights[0], weights[2]), inner)
    weights_outer = between(weights[2], outer)
    across_there = swap(across, 1)
    low_there, high_there = swap(low, 1), swap(high, 1)
    early = [(own,), (own_there,), (beside,), (beside_there,), (across,), (across_there,)]
    late = [(low, high), (low_there, high_there)]

    pair_0 = [(weights[0],), (weights[2],)]
    pair_1 = [(weights[1],), (weights_inner, weights_outer)]
    part_0 = states_of(place, pair_0, early) + states_of(place, pair_0, late)
    part_1 = states_of(place, pair_1, early + late)

    key_rows = w_keyval.shape[0]
    middle = (z == 1) | (z == 2)
    mine = jnp.zeros((LAYERS,) + w_query.shape, jnp.bfloat16)
    last = jnp.where(middle, weights_inner[key_rows:], weights_outer[key_rows:])
    for k, rows in enumerate([weights[i][key_rows:] for i in range(3)] + [last]):
        mine = lax.dynamic_update_slice_in_dim(mine, rows[None], z ^ k, axis=0)
    mine = mine.reshape(LAYERS * w_query.shape[0], -1)
    there = swap(mine, 1)
    frame_a, frame_b = queries_of(
        place, mine, there, [(own,), (beside,), (across,), (low, high)]
    )
    frame_before = between(frame_b, {0: 1, 1: 2, 2: 3})
    frame_after = between(frame_a, {1: 0, 2: 1, 3: 2})

    odd = z % 2 == 1
    part = jnp.concatenate([jnp.where(odd, part_1, part_0), jnp.where(odd, part_0, part_1)])
    state = sum(
        send(part, lambda z, slot, k=k: (z ^ k, 2 * (slot % 4) + slot // 4)) for k in range(LAYERS)
    )
    state_there = swap(state, 1)
    by_head = taps.reshape(3, LAYERS, 4, HDIM)
    tap = lax.dynamic_index_in_dim(by_head, chip, axis=2, keepdims=False).reshape(3, -1).T
    pieces = attend(place, state, state_there, tap, (frame_a, frame_b, frame_before, frame_after))
    got = [pieces[0]] + [swap(pieces[k], 2 * k) for k in range(1, 4)]
    return finish(place, got)


def local(tokens, w_query, w_keyval, taps):
    fits = (
        lax.axis_size("frame") == LAYERS * PLANE
        and HEADS == 2 * PLANE
        and w_keyval.shape[0] == HDIM
        and 2 * w_query.shape[0] == HDIM
        and PLANE * tokens.shape[0] == 2 * HEIGHT * WIDTH
    )
    return (planes if fits else gathered)(tokens, w_query, w_keyval, taps)


def solution(mesh):
    placed = (P(("grp", "frame"), None), P("frame", None), P("frame", None), P())
    return jax.shard_map(
        local, mesh=mesh, in_specs=placed, out_specs=P(("grp", "frame"), None), check_vma=False
    )
```

```python
import functools

import jax
import jax.numpy as jnp
from jax import lax
from jax.experimental import pallas as pl
from jax.experimental.pallas import tpu as pltpu
from jax.sharding import PartitionSpec as P

HEADS = 16
HDIM = 112
HEIGHT = 32
WIDTH = 32


epsilon = 1e-06


def from_behind(value, axis, steps):
    count = lax.axis_size(axis)
    leading, last = (max(0, -steps), min(count, count - steps))
    return lax.ppermute(value, axis, [(source, source + steps) for source in range(leading, last)])


def normalize(rows_in):
    values = rows_in.astype(jnp.float32)
    scale_inv = lax.rsqrt(jnp.mean(values * values, axis=-1, keepdims=True) + epsilon)
    return (values * scale_inv).astype(jnp.bfloat16)


def gathered(tokens, w_query, w_keyval, taps):
    channels = HEADS * HDIM
    rows_here = tokens.shape[0]
    normed = normalize(tokens)

    def project_rows(weight_rows):
        return lax.dot_general(
            normed, weight_rows, (((1,), (1,)), ((), ())), preferred_element_type=jnp.float32
        )

    keyval_lin = project_rows(lax.all_gather(w_keyval, "frame", axis=0, tiled=True))
    key_feats = jax.nn.relu(keyval_lin[:, :channels]).astype(jnp.bfloat16)
    value_proj = keyval_lin[:, channels:].astype(jnp.bfloat16)
    key_heads = key_feats.reshape(rows_here, HEADS, HDIM)
    value_heads = value_proj.reshape(rows_here, HEADS, HDIM)
    local_state = jnp.einsum(
        "thd,the->hde", key_heads, value_heads, preferred_element_type=jnp.float32
    )
    local_keys = jnp.sum(key_heads.astype(jnp.float32), axis=0)
    query_lin = project_rows(lax.all_gather(w_query, "frame", axis=0, tiled=True))
    query_feats = jax.nn.relu(query_lin).astype(jnp.bfloat16)
    state, key_total = lax.psum((local_state, local_keys), "frame")
    query_heads = query_feats.reshape(rows_here, HEADS, HDIM).astype(jnp.float32)
    numer = jnp.einsum("thd,hde->the", query_heads, state, precision=lax.Precision.HIGHEST)
    denom = (
        jnp.einsum("thd,hd->th", query_heads, key_total, precision=lax.Precision.HIGHEST) + epsilon
    )
    attended = (numer / denom[:, :, None]).reshape(rows_here, channels).astype(jnp.bfloat16)
    strips = HEIGHT * WIDTH // rows_here
    earlier = from_behind(attended, "frame", strips)
    later_frame = from_behind(attended, "frame", -strips)
    mixed = (
        taps[0] * earlier.astype(jnp.float32)
        + taps[1] * attended.astype(jnp.float32)
        + taps[2] * later_frame.astype(jnp.float32)
    ).astype(jnp.bfloat16)
    return mixed


VMEM = pl.BlockSpec(memory_space=pltpu.VMEM)
SMEM = pl.BlockSpec(memory_space=pltpu.SMEM)
ANY = pl.BlockSpec(memory_space=pl.ANY)
ANY = pl.BlockSpec(memory_space=pl.ANY)
PARAMS = pltpu.CompilerParams(vmem_limit_bytes=16 * 2**20)


def kernel_call(body, outs, *operands, scalars=1, scratch=(), flops=0):
    moved = sum(one.size * one.dtype.itemsize for one in operands)
    return pl.pallas_call(
        body,
        out_shape=outs,
        in_specs=[SMEM] * scalars + [VMEM] * (len(operands) - scalars),
        out_specs=jax.tree.map(lambda _: VMEM, outs),
        scratch_shapes=list(scratch),
        compiler_params=PARAMS,
        cost_estimate=pl.CostEstimate(flops=flops, bytes_accessed=moved, transcendentals=0),
    )(*operands)


def like(shape, dtype=jnp.bfloat16):
    return jax.ShapeDtypeStruct(shape, dtype)


def begin_kernel(tokens, normed):
    depth = tokens.shape[0]
    step = depth // 10
    total = jnp.zeros((1, tokens.shape[1]), jnp.float32)
    for start in range(0, depth, step):
        values = tokens[start : start + step].astype(jnp.float32)
        total += jnp.sum(values * values, axis=0, keepdims=True)
    scale_inv = lax.rsqrt(total / depth + epsilon)
    for start in range(0, depth, step):
        values = tokens[start : start + step].astype(jnp.float32)
        normed[start : start + step] = (values * scale_inv).astype(jnp.bfloat16)


def begin(tokens):
    return kernel_call(begin_kernel, like(tokens.shape), tokens, scalars=0)


def relay_kernel(place, beside, across, out):
    core = place[1] % 2
    for k, block in enumerate((across, beside)):

        @pl.when(core == k)
        def _():
            out[...] = block[...]


def relay(place, beside, across):
    return kernel_call(relay_kernel, like(beside.shape), place, beside, across)


def spaced(rows):
    gap = -rows.shape[0] % 16
    return jnp.concatenate([rows, jnp.zeros((gap, rows.shape[1]), rows.dtype)], axis=0)


def room_of(rows):
    return (rows + 15) // 16 * 16


def weights_kernel(w_keyval, w_query, out, held, sems):
    split = w_keyval.shape[0]
    copies = [
        pltpu.make_async_copy(w_keyval, out.at[pl.ds(0, split)], sems.at[0]),
        pltpu.make_async_copy(w_query, held, sems.at[1]),
    ]
    for copy in copies:
        copy.start()
    copies[1].wait()
    out[split:] = held[...]
    copies[0].wait()


def weights_of(w_keyval, w_query):
    rows, depth = w_keyval.shape[0] + w_query.shape[0], w_query.shape[1]
    return pl.pallas_call(
        weights_kernel,
        out_shape=like((rows, depth)),
        in_specs=[ANY, ANY],
        out_specs=VMEM,
        scratch_shapes=[
            pltpu.VMEM(w_query.shape, w_query.dtype),
            pltpu.SemaphoreType.DMA((2,)),
        ],
        compiler_params=PARAMS,
    )(w_keyval, w_query)


def last_kernel(place, inner, outer, out):
    z = place[0]
    middle = (z == 1) | (z == 2)
    for flag, rows in ((middle, inner), (jnp.logical_not(middle), outer)):

        @pl.when(flag)
        def _():
            out[...] = rows[...]


def last_of(place, inner, outer):
    return kernel_call(last_kernel, like(inner.shape), place, inner, outer)


def add_states(z, totals, lin):
    keys_first = z < 2
    tokens = lin.shape[1]
    ones = (lax.broadcasted_iota(jnp.int32, (16, tokens), 0) == 0).astype(jnp.bfloat16)
    one, two = lin[:HDIM], lin[HDIM:]
    key = jnp.maximum(jnp.where(keys_first, one, two), 0.0).astype(jnp.bfloat16)
    value = jnp.where(keys_first, two, one).astype(jnp.bfloat16)
    return totals + lax.dot_general(
        jnp.concatenate([value, ones], axis=0),
        key,
        (((1,), (1,)), ((), ())),
        preferred_element_type=jnp.float32,
    )


def ready_kernel(*refs):
    *blocks, keyval, keyval_there, query = refs
    own, first, second = range(3)
    room = query.shape[0] // 6
    for i, out in enumerate((keyval, keyval_there)):
        rows = blocks[3 * i : 3 * i + 3]
        for k, one in enumerate((first, own, second)):
            out[HDIM * k : HDIM * (k + 1)] = rows[one][:HDIM]
        for k in range(3):
            at = (3 * i + k) * room
            query[at : at + room] = spaced(rows[k][HDIM:])


def ready_rows(mine, there):
    rows, depth = mine[0].shape
    outs = (like((3 * HDIM, depth)),) * 2 + (like((6 * room_of(rows - HDIM), depth)),)
    return kernel_call(ready_kernel, outs, *mine, *there, scalars=0)


def state_kernel(place, mine, there, *refs):
    *blocks, out = refs
    for i, rows in enumerate((mine, there)):
        total = 0.0
        for block in blocks:
            lin = jnp.dot(rows[HDIM:], block[...], preferred_element_type=jnp.float32)
            total = add_states(place[0], total, lin)
        out[i] = total


def states_of(place, mine, there, blocks):
    depth, tokens = blocks[0].shape
    return kernel_call(
        state_kernel,
        like((2, HDIM + 16, HDIM), jnp.float32),
        place,
        mine,
        there,
        *blocks,
        flops=8 * HDIM * depth * len(blocks) * tokens,
    )


def late_kernel(core, place, part, *refs):
    rows, last, *blocks, out, held, keys, values = refs
    z = place[0]
    odd, keys_first = z % 2 == 1, z < 2
    held[:HDIM] = rows[:HDIM]
    held[HDIM : 2 * HDIM] = last[:HDIM]
    held[2 * HDIM :] = rows[HDIM:]
    tokens = blocks[0].shape[1]
    ones = (lax.broadcasted_iota(jnp.int32, (16, tokens), 0) == 0).astype(jnp.bfloat16)
    contract = (((1,), (1,)), ((), ()))
    for k, block in enumerate(blocks):
        final = k == len(blocks) - 1
        weights = held[...] if final else held[: 2 * HDIM]
        lin = jnp.dot(weights, block[...], preferred_element_type=jnp.float32)
        to = slice(tokens * k, tokens * (k + 1))
        for i in range(2 if final else 1):
            one, two = (lin[HDIM * j : HDIM * (j + 1)] for j in (2 * i, 2 * i + 1))
            key = jnp.maximum(jnp.where(keys_first, one, two), 0.0).astype(jnp.bfloat16)
            value = jnp.where(keys_first, two, one).astype(jnp.bfloat16)
            if i == 0:
                keys[:, to] = key
                values[:HDIM, to] = value
                values[HDIM:, to] = ones
            else:
                value = jnp.concatenate([value, ones], axis=0)
                first = part[core] + lax.dot_general(
                    value, key, contract, preferred_element_type=jnp.float32
                )
    total = lax.dot_general(values[...], keys[...], contract, preferred_element_type=jnp.float32)
    out[0] = jnp.where(odd, total, first)
    out[1] = jnp.where(odd, first, total)


def late_states(core, place, part, rows, last, blocks):
    depth, tokens = blocks[0].shape
    columns = len(blocks) * tokens
    return kernel_call(
        functools.partial(late_kernel, core),
        like(part.shape, part.dtype),
        place,
        part,
        rows,
        last,
        *blocks,
        scratch=[
            pltpu.VMEM((4 * HDIM, depth), jnp.bfloat16),
            pltpu.VMEM((HDIM, columns), jnp.bfloat16),
            pltpu.VMEM((HDIM + 16, columns), jnp.bfloat16),
        ],
        flops=4 * HDIM * depth * (columns + tokens),
    )


def sum_kernel(*refs):
    total = refs[0][...].astype(jnp.float32)
    for one in refs[1:-1]:
        total += one[...].astype(jnp.float32)
    refs[-1][...] = total.astype(refs[-1].dtype)


def sum_of(parts, dtype):
    return kernel_call(sum_kernel, like(parts[0].shape, dtype), *parts, scalars=0)


def query_kernel(place, *refs):
    rows, last, last_there, block_0, block_1, out, held = refs
    z = place[0]
    half = HDIM // 2
    step = room_of(half)
    for i, one in enumerate((last, last_there)):
        at = LAYERS * step * i
        held[at : at + 3 * step] = rows[3 * step * i : 3 * step * (i + 1)]
        held[at + 3 * step : at + 4 * step] = spaced(one[HDIM:])
    tokens = block_0.shape[1]
    for k, block in enumerate((block_0, block_1)):
        lin = jnp.dot(held[...], block[...], preferred_element_type=jnp.float32)
        for i in range(LAYERS):
            one = lin[step * i : step * i + half]
            two = lin[step * (LAYERS + i) : step * (LAYERS + i) + half]
            head = jnp.maximum(jnp.concatenate([one, two], axis=0), 0.0).astype(jnp.bfloat16)
            rows = pl.ds(pl.multiple_of((z ^ i) * HDIM, 16), HDIM)
            out[rows, tokens * k : tokens * (k + 1)] = head


def queries_of(place, rows, blocks):
    depth, tokens = blocks[0].shape
    height = 2 * LAYERS * room_of(HDIM // 2)
    return kernel_call(
        query_kernel,
        like((LAYERS * HDIM, 2 * tokens)),
        place,
        *rows,
        *blocks,
        scratch=[pltpu.VMEM((height, depth), jnp.bfloat16)],
        flops=2 * height * depth * 2 * tokens,
    )


def attend_kernel(row, place, mine, there, taps, center, side, halo, *outs):
    z, slot = place[0], place[1]
    y, core = slot // 4, slot % 2
    tokens = outs[0].shape[1]
    half = HDIM // 2
    halo_later = y == row
    halo_there = jnp.where(halo_later, z < LAYERS - 1, z > 0)
    to = lax.broadcasted_iota(jnp.int32, (HDIM, HDIM), 0)
    column = lax.broadcasted_iota(jnp.int32, (HDIM, HDIM), 1)
    turned = jnp.where(to < half, to + half, to - half)
    order = (column == jnp.where(core == 0, to, turned)).astype(jnp.bfloat16)
    for m in range(LAYERS):
        own, other = mine[m // 2], there[m // 2]
        state = jnp.where(core == m % 2, own, other)
        high = state.astype(jnp.bfloat16)
        low = (state - high.astype(jnp.float32)).astype(jnp.bfloat16)
        both = jnp.concatenate([high, low], axis=0)
        both = jnp.dot(both, order, preferred_element_type=jnp.float32).astype(jnp.bfloat16)
        rows = pl.ds(HDIM * m, HDIM)

        def attended(frame):
            sums = jnp.dot(both, frame[rows], preferred_element_type=jnp.float32)
            sums = sums[: HDIM + 16] + sums[HDIM + 16 :]
            result = sums[:HDIM] * (1.0 / (sums[HDIM : HDIM + 1] + epsilon))
            return result.astype(jnp.bfloat16).astype(jnp.float32)

        tap = taps[rows]
        tap_side = jnp.where(halo_later, tap[:, 0:1], tap[:, 2:3])
        tap_halo = jnp.where(halo_later, tap[:, 2:3], tap[:, 0:1])
        mixed = tap_side * attended(side) + tap[:, 1:2] * attended(center)
        mixed += tap_halo * jnp.where(halo_there, attended(halo), 0.0)
        for i, out in enumerate(outs):
            out[rows] = mixed[:, tokens * i : tokens * (i + 1)].astype(jnp.bfloat16)


def attend(row, place, mine, there, taps, *frames):
    channels, tokens = frames[0].shape
    outs = (like((channels, tokens // 2)),) * 2
    body = functools.partial(attend_kernel, row)
    return kernel_call(body, outs, place, mine, there, taps, *frames)


def finish_kernel(place, *refs):
    parts, (out, held) = refs[:4], refs[4:]
    chip = place[1] // 2
    tokens = out.shape[0]
    for k, part in enumerate(parts):
        for m in range(LAYERS):
            to = pl.multiple_of((4 * m + (chip ^ k)) * HDIM, 16)
            held[pl.ds(to, HDIM)] = part[pl.ds(HDIM * m, HDIM)]
    row = lax.broadcasted_iota(jnp.int32, (tokens, tokens), 0)
    column = lax.broadcasted_iota(jnp.int32, (tokens, tokens), 1)
    same = (row == column).astype(jnp.bfloat16)
    step = 256
    for at in range(0, out.shape[1], step):
        out[:, at : at + step] = lax.dot_general(
            same, held[at : at + step], (((1,), (1,)), ((), ())), preferred_element_type=jnp.float32
        ).astype(jnp.bfloat16)


def finish(place, parts):
    channels, tokens = parts[0].shape
    return kernel_call(
        finish_kernel,
        like((tokens, 4 * channels)),
        place,
        *parts,
        scratch=[pltpu.VMEM((4 * channels, tokens), jnp.bfloat16)],
    )


STATE_SENT = jnp.bfloat16
LAYERS = 4
PLANE = 8


def send(value, place):
    pairs = []
    for z in range(LAYERS):
        for slot in range(PLANE):
            to = place(z, slot)
            if to is not None:
                pairs.append((z * PLANE + slot, to[0] * PLANE + to[1]))
    return lax.ppermute(value, "frame", pairs)


def swap(value, bits):
    return send(value, lambda z, slot: (z, slot ^ bits))


def between(value, steps):
    return send(value, lambda z, slot: (steps[z], slot) if z in steps else None)


def together(*values):
    return lax.optimization_barrier(values)


def planes(tokens, w_query, w_keyval, taps):
    me = lax.axis_index("frame")
    z, slot = me // PLANE, me % PLANE
    chip = slot // 2
    place = jnp.stack([z, slot]).astype(jnp.int32)

    cross = [{i: i ^ k for i in range(LAYERS)} for k in range(LAYERS)]
    inner, outer = {1: 2, 2: 1}, {1: 0, 2: 3}

    by_head = taps.reshape(3, LAYERS, 4, HDIM)
    tap = lax.dynamic_index_in_dim(by_head, chip, axis=2, keepdims=False).reshape(3, -1).T
    weights = weights_of(w_keyval, w_query)
    weights_2 = between(weights, cross[2])
    weights_1 = between(weights, cross[1])
    own = begin(tokens.T)
    beside, across = swap(own, 2), swap(own, 4)
    weights_there = swap(weights, 1)
    own, beside, across, weights, weights_1, weights_2, weights_there, tap = together(
        own, beside, across, weights, weights_1, weights_2, weights_there, tap
    )

    weights_inner = between(weights, inner)
    weights_outer = between(weights_2, outer)
    passed = relay(place, beside, across)
    diagonal = send(passed, lambda z, slot: (z, slot ^ (4 if slot % 2 else 2)))
    there_2, there_1 = swap(weights_2, 1), swap(weights_1, 1)
    keyval, keyval_there, query = ready_rows(
        (weights, weights_1, weights_2), (weights_there, there_1, there_2)
    )
    part = states_of(place, keyval, keyval_there, (own, beside, across))
    diagonal, weights_inner, weights_outer, part = together(
        diagonal, weights_inner, weights_outer, part
    )

    weights_3 = last_of(place, weights_inner, weights_outer)
    there_3 = swap(weights_3, 1)
    blocks = (own, beside, across, diagonal)
    kept = late_states(0, place, part, keyval, weights_3, blocks)
    rows = (query, weights_3, there_3)
    here = queries_of(place, rows, (own, beside))
    there = queries_of(place, rows, (across, diagonal))
    there, part = together(there, part)
    given = late_states(1, place, part, keyval_there, there_3, blocks)
    part = sum_of([kept, swap(given, 1)], STATE_SENT)
    part = send(part, lambda z, slot: (z, 2 * (slot % 4) + slot // 4))
    state = sum_of([part] + [between(part, cross[k]) for k in range(1, LAYERS)], jnp.float32)
    state_there = swap(state, 1)

    def aside(value, row):
        def to(z, slot):
            z += 1 if slot // 4 == row else -1
            return (z, slot) if 0 <= z < LAYERS else None

        return send(value, to)


    halo_there, halo_here = aside(here, 1), aside(there, 0)
    out_across = attend(0, place, state, state_there, tap, there, here, halo_there)
    got_across = swap(out_across[0], 4), swap(out_across[1], 6)
    out_here = attend(1, place, state, state_there, tap, here, there, halo_here)
    got_beside = swap(out_here[1], 2)
    return finish(place, [out_here[0], got_beside, *got_across])


def local(tokens, w_query, w_keyval, taps):
    fits = (
        lax.axis_size("frame") == LAYERS * PLANE
        and HEADS == 2 * PLANE
        and w_keyval.shape[0] == HDIM
        and 2 * w_query.shape[0] == HDIM
        and PLANE * tokens.shape[0] == 2 * HEIGHT * WIDTH
    )
    return (planes if fits else gathered)(tokens, w_query, w_keyval, taps)


def solution(mesh):
    placed = (P(("grp", "frame"), None), P("frame", None), P("frame", None), P())
    return jax.shard_map(
        local, mesh=mesh, in_specs=placed, out_specs=P(("grp", "frame"), None), check_vma=False
    )
```

```python
import functools

import jax
import jax.numpy as jnp
from jax import lax
from jax.experimental import pallas as pl
from jax.experimental.pallas import tpu as pltpu
from jax.sharding import PartitionSpec as P

HEADS = 16
HDIM = 112
HEIGHT = 32
WIDTH = 32


epsilon = 1e-06


def from_behind(value, axis, steps):
    count = lax.axis_size(axis)
    leading, last = (max(0, -steps), min(count, count - steps))
    return lax.ppermute(value, axis, [(source, source + steps) for source in range(leading, last)])


def normalize(rows_in):
    values = rows_in.astype(jnp.float32)
    scale_inv = lax.rsqrt(jnp.mean(values * values, axis=-1, keepdims=True) + epsilon)
    return (values * scale_inv).astype(jnp.bfloat16)


def gathered(tokens, w_query, w_keyval, taps):
    channels = HEADS * HDIM
    rows_here = tokens.shape[0]
    normed = normalize(tokens)

    def project_rows(weight_rows):
        return lax.dot_general(
            normed, weight_rows, (((1,), (1,)), ((), ())), preferred_element_type=jnp.float32
        )

    keyval_lin = project_rows(lax.all_gather(w_keyval, "frame", axis=0, tiled=True))
    key_feats = jax.nn.relu(keyval_lin[:, :channels]).astype(jnp.bfloat16)
    value_proj = keyval_lin[:, channels:].astype(jnp.bfloat16)
    key_heads = key_feats.reshape(rows_here, HEADS, HDIM)
    value_heads = value_proj.reshape(rows_here, HEADS, HDIM)
    local_state = jnp.einsum(
        "thd,the->hde", key_heads, value_heads, preferred_element_type=jnp.float32
    )
    local_keys = jnp.sum(key_heads.astype(jnp.float32), axis=0)
    query_lin = project_rows(lax.all_gather(w_query, "frame", axis=0, tiled=True))
    query_feats = jax.nn.relu(query_lin).astype(jnp.bfloat16)
    state, key_total = lax.psum((local_state, local_keys), "frame")
    query_heads = query_feats.reshape(rows_here, HEADS, HDIM).astype(jnp.float32)
    numer = jnp.einsum("thd,hde->the", query_heads, state, precision=lax.Precision.HIGHEST)
    denom = (
        jnp.einsum("thd,hd->th", query_heads, key_total, precision=lax.Precision.HIGHEST) + epsilon
    )
    attended = (numer / denom[:, :, None]).reshape(rows_here, channels).astype(jnp.bfloat16)
    strips = HEIGHT * WIDTH // rows_here
    earlier = from_behind(attended, "frame", strips)
    later_frame = from_behind(attended, "frame", -strips)
    mixed = (
        taps[0] * earlier.astype(jnp.float32)
        + taps[1] * attended.astype(jnp.float32)
        + taps[2] * later_frame.astype(jnp.float32)
    ).astype(jnp.bfloat16)
    return mixed


VMEM = pl.BlockSpec(memory_space=pltpu.VMEM)
SMEM = pl.BlockSpec(memory_space=pltpu.SMEM)
ANY = pl.BlockSpec(memory_space=pl.ANY)
ANY = pl.BlockSpec(memory_space=pl.ANY)
PARAMS = pltpu.CompilerParams(vmem_limit_bytes=16 * 2**20)


def kernel_call(body, outs, *operands, scalars=1, scratch=(), flops=0):
    moved = sum(one.size * one.dtype.itemsize for one in operands)
    return pl.pallas_call(
        body,
        out_shape=outs,
        in_specs=[SMEM] * scalars + [VMEM] * (len(operands) - scalars),
        out_specs=jax.tree.map(lambda _: VMEM, outs),
        scratch_shapes=list(scratch),
        compiler_params=PARAMS,
        cost_estimate=pl.CostEstimate(flops=flops, bytes_accessed=moved, transcendentals=0),
    )(*operands)


def like(shape, dtype=jnp.bfloat16):
    return jax.ShapeDtypeStruct(shape, dtype)


def begin_kernel(tokens, normed):
    depth = tokens.shape[0]
    step = depth // 10
    total = jnp.zeros((1, tokens.shape[1]), jnp.float32)
    for start in range(0, depth, step):
        values = tokens[start : start + step].astype(jnp.float32)
        total += jnp.sum(values * values, axis=0, keepdims=True)
    scale_inv = lax.rsqrt(total / depth + epsilon)
    for start in range(0, depth, step):
        values = tokens[start : start + step].astype(jnp.float32)
        normed[start : start + step] = (values * scale_inv).astype(jnp.bfloat16)


def begin(tokens):
    return kernel_call(begin_kernel, like(tokens.shape), tokens, scalars=0)


def relay_kernel(place, beside, across, out):
    core = place[1] % 2
    for k, block in enumerate((across, beside)):

        @pl.when(core == k)
        def _():
            out[...] = block[...]


def relay(place, beside, across):
    return kernel_call(relay_kernel, like(beside.shape), place, beside, across)


def spaced(rows):
    gap = -rows.shape[0] % 16
    return jnp.concatenate([rows, jnp.zeros((gap, rows.shape[1]), rows.dtype)], axis=0)


def room_of(rows):
    return (rows + 15) // 16 * 16


def weights_kernel(w_keyval, w_query, out, held, sems):
    split = w_keyval.shape[0]
    copies = [
        pltpu.make_async_copy(w_keyval, out.at[pl.ds(0, split)], sems.at[0]),
        pltpu.make_async_copy(w_query, held, sems.at[1]),
    ]
    for copy in copies:
        copy.start()
    copies[1].wait()
    out[split:] = held[...]
    copies[0].wait()


def weights_of(w_keyval, w_query):
    rows, depth = w_keyval.shape[0] + w_query.shape[0], w_query.shape[1]
    return pl.pallas_call(
        weights_kernel,
        out_shape=like((rows, depth)),
        in_specs=[ANY, ANY],
        out_specs=VMEM,
        scratch_shapes=[
            pltpu.VMEM(w_query.shape, w_query.dtype),
            pltpu.SemaphoreType.DMA((2,)),
        ],
        compiler_params=PARAMS,
    )(w_keyval, w_query)


def last_kernel(place, inner, outer, out):
    z = place[0]
    middle = (z == 1) | (z == 2)
    for flag, rows in ((middle, inner), (jnp.logical_not(middle), outer)):

        @pl.when(flag)
        def _():
            out[...] = rows[...]


def last_of(place, inner, outer):
    return kernel_call(last_kernel, like(inner.shape), place, inner, outer)


def add_states(z, totals, lin):
    keys_first = z < 2
    tokens = lin.shape[1]
    ones = (lax.broadcasted_iota(jnp.int32, (16, tokens), 0) == 0).astype(jnp.bfloat16)
    one, two = lin[:HDIM], lin[HDIM:]
    key = jnp.maximum(jnp.where(keys_first, one, two), 0.0).astype(jnp.bfloat16)
    value = jnp.where(keys_first, two, one).astype(jnp.bfloat16)
    return totals + lax.dot_general(
        jnp.concatenate([value, ones], axis=0),
        key,
        (((1,), (1,)), ((), ())),
        preferred_element_type=jnp.float32,
    )


def ready_kernel(*refs):
    *blocks, keyval, keyval_there, query = refs
    own, first, second = range(3)
    room = query.shape[0] // 6
    for i, out in enumerate((keyval, keyval_there)):
        rows = blocks[3 * i : 3 * i + 3]
        for k, one in enumerate((first, own, second)):
            out[HDIM * k : HDIM * (k + 1)] = rows[one][:HDIM]
        for k in range(3):
            at = (3 * i + k) * room
            query[at : at + room] = spaced(rows[k][HDIM:])


def ready_rows(mine, there):
    rows, depth = mine[0].shape
    outs = (like((3 * HDIM, depth)),) * 2 + (like((6 * room_of(rows - HDIM), depth)),)
    return kernel_call(ready_kernel, outs, *mine, *there, scalars=0)


def state_kernel(place, mine, there, *refs):
    *blocks, out = refs
    for i, rows in enumerate((mine, there)):
        total = 0.0
        for block in blocks:
            lin = jnp.dot(rows[HDIM:], block[...], preferred_element_type=jnp.float32)
            total = add_states(place[0], total, lin)
        out[i] = total


def states_of(place, mine, there, blocks):
    depth, tokens = blocks[0].shape
    return kernel_call(
        state_kernel,
        like((2, HDIM + 16, HDIM), jnp.float32),
        place,
        mine,
        there,
        *blocks,
        flops=8 * HDIM * depth * len(blocks) * tokens,
    )


def late_kernel(core, place, part, rows, last, *refs):
    *blocks, out, held, keys, values = refs
    z = place[0]
    odd, keys_first = z % 2 == 1, z < 2
    held[:HDIM] = rows[:HDIM]
    held[HDIM:] = last[:HDIM]
    tokens = blocks[0].shape[1]
    ones = (lax.broadcasted_iota(jnp.int32, (16, tokens), 0) == 0).astype(jnp.bfloat16)
    for k, block in enumerate(blocks):
        lin = jnp.dot(held[...], block[...], preferred_element_type=jnp.float32)
        to = slice(tokens * k, tokens * (k + 1))
        one, two = lin[:HDIM], lin[HDIM:]
        key = jnp.maximum(jnp.where(keys_first, one, two), 0.0)
        keys[:, to] = key.astype(jnp.bfloat16)
        values[:HDIM, to] = jnp.where(keys_first, two, one).astype(jnp.bfloat16)
        values[HDIM:, to] = ones
    total = lax.dot_general(
        values[...], keys[...], (((1,), (1,)), ((), ())), preferred_element_type=jnp.float32
    )
    out[0] = jnp.where(odd, total, part[core])
    out[1] = jnp.where(odd, part[core], total)


def late_states(core, place, part, rows, last, blocks):
    depth, tokens = blocks[0].shape
    columns = len(blocks) * tokens
    return kernel_call(
        functools.partial(late_kernel, core),
        like(part.shape, part.dtype),
        place,
        part,
        rows,
        last,
        *blocks,
        scratch=[
            pltpu.VMEM((2 * HDIM, depth), jnp.bfloat16),
            pltpu.VMEM((HDIM, columns), jnp.bfloat16),
            pltpu.VMEM((HDIM + 16, columns), jnp.bfloat16),
        ],
        flops=4 * HDIM * depth * columns,
    )


def sum_kernel(*refs):
    total = refs[0][...].astype(jnp.float32)
    for one in refs[1:-1]:
        total += one[...].astype(jnp.float32)
    refs[-1][...] = total.astype(refs[-1].dtype)


def sum_of(parts, dtype):
    return kernel_call(sum_kernel, like(parts[0].shape, dtype), *parts, scalars=0)


def query_heads(z, lin, first, one, two, out, columns):
    half = HDIM // 2
    head = jnp.concatenate([lin[one : one + half], lin[two : two + half]], axis=0)
    rows = pl.ds(pl.multiple_of((z ^ first) * HDIM, 16), HDIM)
    out[rows, columns] = jnp.maximum(head, 0.0).astype(jnp.bfloat16)


def near_query_kernel(place, rows, *refs):
    *blocks, out = refs
    step = rows.shape[0] // 6
    tokens = blocks[0].shape[1]
    for k, block in enumerate(blocks):
        lin = jnp.dot(rows[...], block[...], preferred_element_type=jnp.float32)
        for i in range(3):
            columns = slice(tokens * k, tokens * (k + 1))
            query_heads(place[0], lin, i, step * i, step * (3 + i), out, columns)


def near_queries(place, rows, blocks):
    tokens = blocks[0].shape[1]
    return kernel_call(
        near_query_kernel, like((LAYERS * HDIM, len(blocks) * tokens)), place, rows, *blocks
    )


def query_kernel(place, near, last, last_there, block_0, block_1, out, held):
    step = held.shape[0] // 2
    held[:step] = spaced(last[HDIM:])
    held[step:] = spaced(last_there[HDIM:])
    out[...] = near[...]
    tokens = block_0.shape[1]
    for k, block in enumerate((block_0, block_1)):
        lin = jnp.dot(held[...], block[...], preferred_element_type=jnp.float32)
        columns = slice(tokens * k, tokens * (k + 1))
        query_heads(place[0], lin, 3, 0, step, out, columns)


def queries_of(place, near, rows, blocks):
    depth = blocks[0].shape[0]
    return kernel_call(
        query_kernel,
        like(near.shape),
        place,
        near,
        *rows,
        *blocks,
        scratch=[pltpu.VMEM((2 * room_of(HDIM // 2), depth), jnp.bfloat16)],
    )


def attend_kernel(row, place, mine, there, taps, center, side, halo, *outs):
    z, slot = place[0], place[1]
    y, core = slot // 4, slot % 2
    tokens = outs[0].shape[1]
    half = HDIM // 2
    halo_later = y == row
    halo_there = jnp.where(halo_later, z < LAYERS - 1, z > 0)
    to = lax.broadcasted_iota(jnp.int32, (HDIM, HDIM), 0)
    column = lax.broadcasted_iota(jnp.int32, (HDIM, HDIM), 1)
    turned = jnp.where(to < half, to + half, to - half)
    order = (column == jnp.where(core == 0, to, turned)).astype(jnp.bfloat16)
    for m in range(LAYERS):
        own, other = mine[m // 2], there[m // 2]
        state = jnp.where(core == m % 2, own, other)
        high = state.astype(jnp.bfloat16)
        low = (state - high.astype(jnp.float32)).astype(jnp.bfloat16)
        both = jnp.concatenate([high, low], axis=0)
        both = jnp.dot(both, order, preferred_element_type=jnp.float32).astype(jnp.bfloat16)
        rows = pl.ds(HDIM * m, HDIM)

        def attended(frame):
            sums = jnp.dot(both, frame[rows], preferred_element_type=jnp.float32)
            sums = sums[: HDIM + 16] + sums[HDIM + 16 :]
            result = sums[:HDIM] * (1.0 / (sums[HDIM : HDIM + 1] + epsilon))
            return result.astype(jnp.bfloat16).astype(jnp.float32)

        tap = taps[rows]
        tap_side = jnp.where(halo_later, tap[:, 0:1], tap[:, 2:3])
        tap_halo = jnp.where(halo_later, tap[:, 2:3], tap[:, 0:1])
        mixed = tap_side * attended(side) + tap[:, 1:2] * attended(center)
        mixed += tap_halo * jnp.where(halo_there, attended(halo), 0.0)
        for i, out in enumerate(outs):
            out[rows] = mixed[:, tokens * i : tokens * (i + 1)].astype(jnp.bfloat16)


def attend(row, place, mine, there, taps, *frames):
    channels, tokens = frames[0].shape
    outs = (like((channels, tokens // 2)),) * 2
    body = functools.partial(attend_kernel, row)
    return kernel_call(body, outs, place, mine, there, taps, *frames)


def finish_kernel(place, *refs):
    parts, (out, held) = refs[:4], refs[4:]
    chip = place[1] // 2
    tokens = out.shape[0]
    for k, part in enumerate(parts):
        for m in range(LAYERS):
            to = pl.multiple_of((4 * m + (chip ^ k)) * HDIM, 16)
            held[pl.ds(to, HDIM)] = part[pl.ds(HDIM * m, HDIM)]
    row = lax.broadcasted_iota(jnp.int32, (tokens, tokens), 0)
    column = lax.broadcasted_iota(jnp.int32, (tokens, tokens), 1)
    same = (row == column).astype(jnp.bfloat16)
    step = 256
    for at in range(0, out.shape[1], step):
        out[:, at : at + step] = lax.dot_general(
            same, held[at : at + step], (((1,), (1,)), ((), ())), preferred_element_type=jnp.float32
        ).astype(jnp.bfloat16)


def finish(place, parts):
    channels, tokens = parts[0].shape
    return kernel_call(
        finish_kernel,
        like((tokens, 4 * channels)),
        place,
        *parts,
        scratch=[pltpu.VMEM((4 * channels, tokens), jnp.bfloat16)],
    )


STATE_SENT = jnp.bfloat16
LAYERS = 4
PLANE = 8


def send(value, place):
    pairs = []
    for z in range(LAYERS):
        for slot in range(PLANE):
            to = place(z, slot)
            if to is not None:
                pairs.append((z * PLANE + slot, to[0] * PLANE + to[1]))
    return lax.ppermute(value, "frame", pairs)


def swap(value, bits):
    return send(value, lambda z, slot: (z, slot ^ bits))


def between(value, steps):
    return send(value, lambda z, slot: (steps[z], slot) if z in steps else None)


def together(*values):
    return lax.optimization_barrier(values)


def planes(tokens, w_query, w_keyval, taps):
    me = lax.axis_index("frame")
    z, slot = me // PLANE, me % PLANE
    chip = slot // 2
    place = jnp.stack([z, slot]).astype(jnp.int32)

    cross = [{i: i ^ k for i in range(LAYERS)} for k in range(LAYERS)]
    inner, outer = {1: 2, 2: 1}, {1: 0, 2: 3}

    by_head = taps.reshape(3, LAYERS, 4, HDIM)
    tap = lax.dynamic_index_in_dim(by_head, chip, axis=2, keepdims=False).reshape(3, -1).T
    weights = weights_of(w_keyval, w_query)
    weights_2 = between(weights, cross[2])
    weights_1 = between(weights, cross[1])
    own = begin(tokens.T)
    beside, across = swap(own, 2), swap(own, 4)
    weights_there = swap(weights, 1)
    own, beside, across, weights, weights_1, weights_2, weights_there, tap = together(
        own, beside, across, weights, weights_1, weights_2, weights_there, tap
    )

    weights_inner = between(weights, inner)
    weights_outer = between(weights_2, outer)
    passed = relay(place, beside, across)
    diagonal = send(passed, lambda z, slot: (z, slot ^ (4 if slot % 2 else 2)))
    there_2, there_1 = swap(weights_2, 1), swap(weights_1, 1)
    keyval, keyval_there, query = ready_rows(
        (weights, weights_1, weights_2), (weights_there, there_1, there_2)
    )
    blocks = (own, beside, across, diagonal)
    part = states_of(place, keyval, keyval_there, blocks)
    near_here = near_queries(place, query, (own, beside))
    near_there = near_queries(place, query, (across, diagonal))
    diagonal, weights_inner, weights_outer, part, near_here, near_there = together(
        diagonal, weights_inner, weights_outer, part, near_here, near_there
    )

    weights_3 = last_of(place, weights_inner, weights_outer)
    there_3 = swap(weights_3, 1)
    kept = late_states(0, place, part, keyval, weights_3, blocks)
    given = late_states(1, place, part, keyval_there, there_3, blocks)
    kept, given, near_here = together(kept, given, near_here)
    rows = (weights_3, there_3)
    here = queries_of(place, near_here, rows, (own, beside))
    there = queries_of(place, near_there, rows, (across, diagonal))
    part = sum_of([kept, swap(given, 1)], STATE_SENT)
    parts = [part] + [between(part, cross[k]) for k in range(1, LAYERS)]
    here, parts[1] = together(here, parts[1])
    there, *parts = together(there, *parts)
    state = sum_of(parts, STATE_SENT)
    state, state_there = (
        send(state, lambda z, slot, flip=flip: (z, 2 * (slot % 4) + (slot // 4 ^ flip)))
        for flip in range(2)
    )

    def aside(value, row):
        def to(z, slot):
            z += 1 if slot // 4 == row else -1
            return (z, slot) if 0 <= z < LAYERS else None

        return send(value, to)


    halo_there, halo_here = aside(here, 1), aside(there, 0)
    out_across = attend(0, place, state, state_there, tap, there, here, halo_there)
    got_across = swap(out_across[0], 4), swap(out_across[1], 6)
    out_here = attend(1, place, state, state_there, tap, here, there, halo_here)
    got_beside = swap(out_here[1], 2)
    return finish(place, [out_here[0], got_beside, *got_across])


def local(tokens, w_query, w_keyval, taps):
    fits = (
        lax.axis_size("frame") == LAYERS * PLANE
        and HEADS == 2 * PLANE
        and w_keyval.shape[0] == HDIM
        and 2 * w_query.shape[0] == HDIM
        and PLANE * tokens.shape[0] == 2 * HEIGHT * WIDTH
    )
    return (planes if fits else gathered)(tokens, w_query, w_keyval, taps)


def solution(mesh):
    placed = (P(("grp", "frame"), None), P("frame", None), P("frame", None), P())
    return jax.shard_map(
        local, mesh=mesh, in_specs=placed, out_specs=P(("grp", "frame"), None), check_vma=False
    )
```

```python
import functools

import jax
import jax.numpy as jnp
from jax import lax
from jax.experimental import pallas as pl
from jax.experimental.pallas import tpu as pltpu
from jax.sharding import PartitionSpec as P

HEADS = 16
HDIM = 112
HEIGHT = 32
WIDTH = 32


epsilon = 1e-06


def from_behind(value, axis, steps):
    count = lax.axis_size(axis)
    leading, last = (max(0, -steps), min(count, count - steps))
    return lax.ppermute(value, axis, [(source, source + steps) for source in range(leading, last)])


def normalize(rows_in):
    values = rows_in.astype(jnp.float32)
    scale_inv = lax.rsqrt(jnp.mean(values * values, axis=-1, keepdims=True) + epsilon)
    return (values * scale_inv).astype(jnp.bfloat16)


def gathered(tokens, w_query, w_keyval, taps):
    channels = HEADS * HDIM
    rows_here = tokens.shape[0]
    normed = normalize(tokens)

    def project_rows(weight_rows):
        return lax.dot_general(
            normed, weight_rows, (((1,), (1,)), ((), ())), preferred_element_type=jnp.float32
        )

    keyval_lin = project_rows(lax.all_gather(w_keyval, "frame", axis=0, tiled=True))
    key_feats = jax.nn.relu(keyval_lin[:, :channels]).astype(jnp.bfloat16)
    value_proj = keyval_lin[:, channels:].astype(jnp.bfloat16)
    key_heads = key_feats.reshape(rows_here, HEADS, HDIM)
    value_heads = value_proj.reshape(rows_here, HEADS, HDIM)
    local_state = jnp.einsum(
        "thd,the->hde", key_heads, value_heads, preferred_element_type=jnp.float32
    )
    local_keys = jnp.sum(key_heads.astype(jnp.float32), axis=0)
    query_lin = project_rows(lax.all_gather(w_query, "frame", axis=0, tiled=True))
    query_feats = jax.nn.relu(query_lin).astype(jnp.bfloat16)
    state, key_total = lax.psum((local_state, local_keys), "frame")
    query_heads = query_feats.reshape(rows_here, HEADS, HDIM).astype(jnp.float32)
    numer = jnp.einsum("thd,hde->the", query_heads, state, precision=lax.Precision.HIGHEST)
    denom = (
        jnp.einsum("thd,hd->th", query_heads, key_total, precision=lax.Precision.HIGHEST) + epsilon
    )
    attended = (numer / denom[:, :, None]).reshape(rows_here, channels).astype(jnp.bfloat16)
    strips = HEIGHT * WIDTH // rows_here
    earlier = from_behind(attended, "frame", strips)
    later_frame = from_behind(attended, "frame", -strips)
    mixed = (
        taps[0] * earlier.astype(jnp.float32)
        + taps[1] * attended.astype(jnp.float32)
        + taps[2] * later_frame.astype(jnp.float32)
    ).astype(jnp.bfloat16)
    return mixed


VMEM = pl.BlockSpec(memory_space=pltpu.VMEM)
SMEM = pl.BlockSpec(memory_space=pltpu.SMEM)
ANY = pl.BlockSpec(memory_space=pl.ANY)
ANY = pl.BlockSpec(memory_space=pl.ANY)
PARAMS = pltpu.CompilerParams(vmem_limit_bytes=16 * 2**20)


def kernel_call(body, outs, *operands, scalars=1, scratch=(), flops=0):
    moved = sum(one.size * one.dtype.itemsize for one in operands)
    return pl.pallas_call(
        body,
        out_shape=outs,
        in_specs=[SMEM] * scalars + [VMEM] * (len(operands) - scalars),
        out_specs=jax.tree.map(lambda _: VMEM, outs),
        scratch_shapes=list(scratch),
        compiler_params=PARAMS,
        cost_estimate=pl.CostEstimate(flops=flops, bytes_accessed=moved, transcendentals=0),
    )(*operands)


def like(shape, dtype=jnp.bfloat16):
    return jax.ShapeDtypeStruct(shape, dtype)


def begin_kernel(tokens, normed):
    depth = tokens.shape[0]
    step = depth // 10
    total = jnp.zeros((1, tokens.shape[1]), jnp.float32)
    for start in range(0, depth, step):
        values = tokens[start : start + step].astype(jnp.float32)
        total += jnp.sum(values * values, axis=0, keepdims=True)
    scale_inv = lax.rsqrt(total / depth + epsilon)
    for start in range(0, depth, step):
        values = tokens[start : start + step].astype(jnp.float32)
        normed[start : start + step] = (values * scale_inv).astype(jnp.bfloat16)


def begin(tokens):
    return kernel_call(begin_kernel, like(tokens.shape), tokens, scalars=0)


def relay_kernel(place, beside, across, out):
    core = place[1] % 2
    for k, block in enumerate((across, beside)):

        @pl.when(core == k)
        def _():
            out[...] = block[...]


def relay(place, beside, across):
    return kernel_call(relay_kernel, like(beside.shape), place, beside, across)


def spaced(rows):
    gap = -rows.shape[0] % 16
    return jnp.concatenate([rows, jnp.zeros((gap, rows.shape[1]), rows.dtype)], axis=0)


def room_of(rows):
    return (rows + 15) // 16 * 16


def weights_kernel(w_keyval, w_query, out, held, sems):
    split = w_keyval.shape[0]
    copies = [
        pltpu.make_async_copy(w_keyval, out.at[pl.ds(0, split)], sems.at[0]),
        pltpu.make_async_copy(w_query, held, sems.at[1]),
    ]
    for copy in copies:
        copy.start()
    copies[1].wait()
    out[split:] = held[...]
    copies[0].wait()


def weights_of(w_keyval, w_query):
    rows, depth = w_keyval.shape[0] + w_query.shape[0], w_query.shape[1]
    return pl.pallas_call(
        weights_kernel,
        out_shape=like((rows, depth)),
        in_specs=[ANY, ANY],
        out_specs=VMEM,
        scratch_shapes=[
            pltpu.VMEM(w_query.shape, w_query.dtype),
            pltpu.SemaphoreType.DMA((2,)),
        ],
        compiler_params=PARAMS,
    )(w_keyval, w_query)


def last_kernel(place, inner, outer, out):
    z = place[0]
    middle = (z == 1) | (z == 2)
    for flag, rows in ((middle, inner), (jnp.logical_not(middle), outer)):

        @pl.when(flag)
        def _():
            out[...] = rows[...]


def last_of(place, inner, outer):
    return kernel_call(last_kernel, like(inner.shape), place, inner, outer)


def add_states(z, totals, lin):
    keys_first = z < 2
    tokens = lin.shape[1]
    ones = (lax.broadcasted_iota(jnp.int32, (16, tokens), 0) == 0).astype(jnp.bfloat16)
    one, two = lin[:HDIM], lin[HDIM:]
    key = jnp.maximum(jnp.where(keys_first, one, two), 0.0).astype(jnp.bfloat16)
    value = jnp.where(keys_first, two, one).astype(jnp.bfloat16)
    return totals + lax.dot_general(
        jnp.concatenate([value, ones], axis=0),
        key,
        (((1,), (1,)), ((), ())),
        preferred_element_type=jnp.float32,
    )


def ready_kernel(*refs):
    *blocks, keyval, keyval_there, query = refs
    own, first, second = range(3)
    room = query.shape[0] // 6
    for i, out in enumerate((keyval, keyval_there)):
        rows = blocks[3 * i : 3 * i + 3]
        for k, one in enumerate((first, own, second)):
            out[HDIM * k : HDIM * (k + 1)] = rows[one][:HDIM]
        for k in range(3):
            at = (3 * i + k) * room
            query[at : at + room] = spaced(rows[k][HDIM:])


def ready_rows(mine, there):
    rows, depth = mine[0].shape
    outs = (like((3 * HDIM, depth)),) * 2 + (like((6 * room_of(rows - HDIM), depth)),)
    return kernel_call(ready_kernel, outs, *mine, *there, scalars=0)


def state_kernel(place, mine, there, *refs):
    *blocks, out = refs
    for i, rows in enumerate((mine, there)):
        total = 0.0
        for block in blocks:
            lin = jnp.dot(rows[HDIM:], block[...], preferred_element_type=jnp.float32)
            total = add_states(place[0], total, lin)
        out[i] = total


def states_of(place, mine, there, blocks):
    depth, tokens = blocks[0].shape
    return kernel_call(
        state_kernel,
        like((2, HDIM + 16, HDIM), jnp.float32),
        place,
        mine,
        there,
        *blocks,
        flops=8 * HDIM * depth * len(blocks) * tokens,
    )


def late_kernel(core, place, part, rows, last, *refs):
    *blocks, out, held, keys, values = refs
    z = place[0]
    odd, keys_first = z % 2 == 1, z < 2
    held[:HDIM] = rows[:HDIM]
    held[HDIM:] = last[:HDIM]
    tokens = blocks[0].shape[1]
    ones = (lax.broadcasted_iota(jnp.int32, (16, tokens), 0) == 0).astype(jnp.bfloat16)
    for k, block in enumerate(blocks):
        lin = jnp.dot(held[...], block[...], preferred_element_type=jnp.float32)
        to = slice(tokens * k, tokens * (k + 1))
        one, two = lin[:HDIM], lin[HDIM:]
        key = jnp.maximum(jnp.where(keys_first, one, two), 0.0)
        keys[:, to] = key.astype(jnp.bfloat16)
        values[:HDIM, to] = jnp.where(keys_first, two, one).astype(jnp.bfloat16)
        values[HDIM:, to] = ones
    total = lax.dot_general(
        values[...], keys[...], (((1,), (1,)), ((), ())), preferred_element_type=jnp.float32
    )
    out[0] = jnp.where(odd, total, part[core])
    out[1] = jnp.where(odd, part[core], total)


def late_states(core, place, part, rows, last, blocks):
    depth, tokens = blocks[0].shape
    columns = len(blocks) * tokens
    return kernel_call(
        functools.partial(late_kernel, core),
        like(part.shape, part.dtype),
        place,
        part,
        rows,
        last,
        *blocks,
        scratch=[
            pltpu.VMEM((2 * HDIM, depth), jnp.bfloat16),
            pltpu.VMEM((HDIM, columns), jnp.bfloat16),
            pltpu.VMEM((HDIM + 16, columns), jnp.bfloat16),
        ],
        flops=4 * HDIM * depth * columns,
    )


def sum_kernel(*refs):
    total = refs[0][...].astype(jnp.float32)
    for one in refs[1:-1]:
        total += one[...].astype(jnp.float32)
    refs[-1][...] = total.astype(refs[-1].dtype)


def sum_of(parts, dtype):
    return kernel_call(sum_kernel, like(parts[0].shape, dtype), *parts, scalars=0)


def query_heads(place, lin, first, one, two, out, columns):
    half = HDIM // 2
    one, two = lin[one : one + half], lin[two : two + half]
    turned = place[1] % 2 == 1
    head = [jnp.where(turned, two, one), jnp.where(turned, one, two)]
    head = jnp.concatenate(head, axis=0)
    rows = pl.ds(pl.multiple_of((place[0] ^ first) * HDIM, 16), HDIM)
    out[rows, columns] = jnp.maximum(head, 0.0).astype(jnp.bfloat16)


def near_query_kernel(place, rows, *refs):
    *blocks, out = refs
    step = rows.shape[0] // 6
    tokens = blocks[0].shape[1]
    for k, block in enumerate(blocks):
        lin = jnp.dot(rows[...], block[...], preferred_element_type=jnp.float32)
        for i in range(3):
            columns = slice(tokens * k, tokens * (k + 1))
            query_heads(place, lin, i, step * i, step * (3 + i), out, columns)


def near_queries(place, rows, blocks):
    tokens = blocks[0].shape[1]
    return kernel_call(
        near_query_kernel, like((LAYERS * HDIM, len(blocks) * tokens)), place, rows, *blocks
    )


def query_kernel(place, near, last, last_there, block_0, block_1, out, held):
    step = held.shape[0] // 2
    held[:step] = spaced(last[HDIM:])
    held[step:] = spaced(last_there[HDIM:])
    out[...] = near[...]
    tokens = block_0.shape[1]
    for k, block in enumerate((block_0, block_1)):
        lin = jnp.dot(held[...], block[...], preferred_element_type=jnp.float32)
        columns = slice(tokens * k, tokens * (k + 1))
        query_heads(place, lin, 3, 0, step, out, columns)


def queries_of(place, near, rows, blocks):
    depth = blocks[0].shape[0]
    return kernel_call(
        query_kernel,
        like(near.shape),
        place,
        near,
        *rows,
        *blocks,
        scratch=[pltpu.VMEM((2 * room_of(HDIM // 2), depth), jnp.bfloat16)],
    )


def attend_kernel(row, strip, place, mine, there, taps, center, side, halo, out):
    z, slot = place[0], place[1]
    y, core = slot // 4, slot % 2
    tokens = out.shape[1]
    columns = slice(tokens * strip, tokens * (strip + 1))
    halo_later = y == row
    halo_there = jnp.where(halo_later, z < LAYERS - 1, z > 0)
    for m in range(LAYERS):
        own, other = mine[m // 2], there[m // 2]
        state = jnp.where(core == m % 2, own, other).astype(jnp.bfloat16)
        rows = pl.ds(HDIM * m, HDIM)

        def attended(frame):
            sums = jnp.dot(state, frame[rows, columns], preferred_element_type=jnp.float32)
            result = sums[:HDIM] * (1.0 / (sums[HDIM : HDIM + 1] + epsilon))
            return result.astype(jnp.bfloat16).astype(jnp.float32)

        tap = taps[rows]
        tap_side = jnp.where(halo_later, tap[:, 0:1], tap[:, 2:3])
        tap_halo = jnp.where(halo_later, tap[:, 2:3], tap[:, 0:1])
        mixed = tap_side * attended(side) + tap[:, 1:2] * attended(center)
        mixed += tap_halo * jnp.where(halo_there, attended(halo), 0.0)
        out[rows] = mixed.astype(jnp.bfloat16)


def attend(row, strip, place, mine, there, taps, *frames):
    channels, tokens = frames[0].shape
    body = functools.partial(attend_kernel, row, strip)
    return kernel_call(
        body, like((channels, tokens // 2)), place, mine, there, taps, *frames
    )


def finish_kernel(place, *refs):
    parts, (out, held) = refs[:4], refs[4:]
    chip = place[1] // 2
    tokens = out.shape[0]
    for k, part in enumerate(parts):
        for m in range(LAYERS):
            to = pl.multiple_of((4 * m + (chip ^ k)) * HDIM, 16)
            held[pl.ds(to, HDIM)] = part[pl.ds(HDIM * m, HDIM)]
    row = lax.broadcasted_iota(jnp.int32, (tokens, tokens), 0)
    column = lax.broadcasted_iota(jnp.int32, (tokens, tokens), 1)
    same = (row == column).astype(jnp.bfloat16)
    step = 256
    for at in range(0, out.shape[1], step):
        out[:, at : at + step] = lax.dot_general(
            same, held[at : at + step], (((1,), (1,)), ((), ())), preferred_element_type=jnp.float32
        ).astype(jnp.bfloat16)


def finish(place, parts):
    channels, tokens = parts[0].shape
    return kernel_call(
        finish_kernel,
        like((tokens, 4 * channels)),
        place,
        *parts,
        scratch=[pltpu.VMEM((4 * channels, tokens), jnp.bfloat16)],
    )


STATE_SENT = jnp.bfloat16
LAYERS = 4
PLANE = 8


def send(value, place):
    pairs = []
    for z in range(LAYERS):
        for slot in range(PLANE):
            to = place(z, slot)
            if to is not None:
                pairs.append((z * PLANE + slot, to[0] * PLANE + to[1]))
    return lax.ppermute(value, "frame", pairs)


def swap(value, bits):
    return send(value, lambda z, slot: (z, slot ^ bits))


def between(value, steps):
    return send(value, lambda z, slot: (steps[z], slot) if z in steps else None)


def together(*values):
    return lax.optimization_barrier(values)


def planes(tokens, w_query, w_keyval, taps):
    me = lax.axis_index("frame")
    z, slot = me // PLANE, me % PLANE
    chip = slot // 2
    place = jnp.stack([z, slot]).astype(jnp.int32)

    cross = [{i: i ^ k for i in range(LAYERS)} for k in range(LAYERS)]
    inner, outer = {1: 2, 2: 1}, {1: 0, 2: 3}

    by_head = taps.reshape(3, LAYERS, 4, HDIM)
    tap = lax.dynamic_index_in_dim(by_head, chip, axis=2, keepdims=False).reshape(3, -1).T
    weights = weights_of(w_keyval, w_query)
    weights_2 = between(weights, cross[2])
    weights_1 = between(weights, cross[1])
    own = begin(tokens.T)
    beside, across = swap(own, 2), swap(own, 4)
    weights_there = swap(weights, 1)
    own, beside, across, weights, weights_1, weights_2, weights_there, tap = together(
        own, beside, across, weights, weights_1, weights_2, weights_there, tap
    )

    weights_inner = between(weights, inner)
    weights_outer = between(weights_2, outer)
    passed = relay(place, beside, across)
    diagonal = send(passed, lambda z, slot: (z, slot ^ (4 if slot % 2 else 2)))
    there_2, there_1 = swap(weights_2, 1), swap(weights_1, 1)
    keyval, keyval_there, query = ready_rows(
        (weights, weights_1, weights_2), (weights_there, there_1, there_2)
    )
    blocks = (own, beside, across, diagonal)
    part = states_of(place, keyval, keyval_there, blocks)
    near_here = near_queries(place, query, (own, beside))
    near_there = near_queries(place, query, (across, diagonal))
    diagonal, weights_inner, weights_outer, part, near_here, near_there = together(
        diagonal, weights_inner, weights_outer, part, near_here, near_there
    )

    weights_3 = last_of(place, weights_inner, weights_outer)
    there_3 = swap(weights_3, 1)
    kept = late_states(0, place, part, keyval, weights_3, blocks)
    given = late_states(1, place, part, keyval_there, there_3, blocks)
    kept, given, near_here = together(kept, given, near_here)
    rows = (weights_3, there_3)
    here = queries_of(place, near_here, rows, (own, beside))
    there = queries_of(place, near_there, rows, (across, diagonal))
    kept, here = together(kept, here)
    part = sum_of([kept, swap(given, 1)], STATE_SENT)
    parts = [part] + [between(part, cross[k]) for k in range(1, LAYERS)]
    here, parts[1] = together(here, parts[1])
    there, *parts = together(there, *parts)
    state = sum_of(parts, STATE_SENT)
    state, state_there = (
        send(state, lambda z, slot, flip=flip: (z, 2 * (slot % 4) + (slot // 4 ^ flip)))
        for flip in range(2)
    )

    def aside(value, row):
        def to(z, slot):
            z += 1 if slot // 4 == row else -1
            return (z, slot) if 0 <= z < LAYERS else None

        return send(value, to)


    halo_there, halo_here = aside(here, 1), aside(there, 0)
    states = (state, state_there, tap)
    got_across = [
        swap(attend(0, strip, place, *states, there, here, halo_there), 4 + 2 * strip)
        for strip in range(2)
    ]
    got_beside = swap(attend(1, 1, place, *states, here, there, halo_here), 2)
    kept_here = attend(1, 0, place, *states, here, there, halo_here)
    return finish(place, [kept_here, got_beside, *got_across])


def local(tokens, w_query, w_keyval, taps):
    fits = (
        lax.axis_size("frame") == LAYERS * PLANE
        and HEADS == 2 * PLANE
        and w_keyval.shape[0] == HDIM
        and 2 * w_query.shape[0] == HDIM
        and PLANE * tokens.shape[0] == 2 * HEIGHT * WIDTH
    )
    return (planes if fits else gathered)(tokens, w_query, w_keyval, taps)


def solution(mesh):
    placed = (P(("grp", "frame"), None), P("frame", None), P("frame", None), P())
    return jax.shard_map(
        local, mesh=mesh, in_specs=placed, out_specs=P(("grp", "frame"), None), check_vma=False
    )
```

```python
import functools

import jax
import jax.numpy as jnp
from jax import lax
from jax.experimental import pallas as pl
from jax.experimental.pallas import tpu as pltpu
from jax.sharding import PartitionSpec as P

HEADS = 16
HDIM = 112
HEIGHT = 32
WIDTH = 32


epsilon = 1e-06


def from_behind(value, axis, steps):
    count = lax.axis_size(axis)
    leading, last = (max(0, -steps), min(count, count - steps))
    return lax.ppermute(value, axis, [(source, source + steps) for source in range(leading, last)])


def normalize(rows_in):
    values = rows_in.astype(jnp.float32)
    scale_inv = lax.rsqrt(jnp.mean(values * values, axis=-1, keepdims=True) + epsilon)
    return (values * scale_inv).astype(jnp.bfloat16)


def gathered(tokens, w_query, w_keyval, taps):
    channels = HEADS * HDIM
    rows_here = tokens.shape[0]
    normed = normalize(tokens)

    def project_rows(weight_rows):
        return lax.dot_general(
            normed, weight_rows, (((1,), (1,)), ((), ())), preferred_element_type=jnp.float32
        )

    keyval_lin = project_rows(lax.all_gather(w_keyval, "frame", axis=0, tiled=True))
    key_feats = jax.nn.relu(keyval_lin[:, :channels]).astype(jnp.bfloat16)
    value_proj = keyval_lin[:, channels:].astype(jnp.bfloat16)
    key_heads = key_feats.reshape(rows_here, HEADS, HDIM)
    value_heads = value_proj.reshape(rows_here, HEADS, HDIM)
    local_state = jnp.einsum(
        "thd,the->hde", key_heads, value_heads, preferred_element_type=jnp.float32
    )
    local_keys = jnp.sum(key_heads.astype(jnp.float32), axis=0)
    query_lin = project_rows(lax.all_gather(w_query, "frame", axis=0, tiled=True))
    query_feats = jax.nn.relu(query_lin).astype(jnp.bfloat16)
    state, key_total = lax.psum((local_state, local_keys), "frame")
    query_heads = query_feats.reshape(rows_here, HEADS, HDIM).astype(jnp.float32)
    numer = jnp.einsum("thd,hde->the", query_heads, state, precision=lax.Precision.HIGHEST)
    denom = (
        jnp.einsum("thd,hd->th", query_heads, key_total, precision=lax.Precision.HIGHEST) + epsilon
    )
    attended = (numer / denom[:, :, None]).reshape(rows_here, channels).astype(jnp.bfloat16)
    strips = HEIGHT * WIDTH // rows_here
    earlier = from_behind(attended, "frame", strips)
    later_frame = from_behind(attended, "frame", -strips)
    mixed = (
        taps[0] * earlier.astype(jnp.float32)
        + taps[1] * attended.astype(jnp.float32)
        + taps[2] * later_frame.astype(jnp.float32)
    ).astype(jnp.bfloat16)
    return mixed


VMEM = pl.BlockSpec(memory_space=pltpu.VMEM)
SMEM = pl.BlockSpec(memory_space=pltpu.SMEM)
ANY = pl.BlockSpec(memory_space=pl.ANY)
PARAMS = pltpu.CompilerParams(vmem_limit_bytes=16 * 2**20)


def kernel_call(body, outs, *operands, scalars=1, scratch=(), flops=0):
    moved = sum(one.size * one.dtype.itemsize for one in operands)
    return pl.pallas_call(
        body,
        out_shape=outs,
        in_specs=[SMEM] * scalars + [VMEM] * (len(operands) - scalars),
        out_specs=jax.tree.map(lambda _: VMEM, outs),
        scratch_shapes=list(scratch),
        compiler_params=PARAMS,
        cost_estimate=pl.CostEstimate(flops=flops, bytes_accessed=moved, transcendentals=0),
    )(*operands)


def like(shape, dtype=jnp.bfloat16):
    return jax.ShapeDtypeStruct(shape, dtype)


def begin_kernel(tokens, normed):
    depth = tokens.shape[0]
    step = depth // 10
    total = jnp.zeros((1, tokens.shape[1]), jnp.float32)
    for start in range(0, depth, step):
        values = tokens[start : start + step].astype(jnp.float32)
        total += jnp.sum(values * values, axis=0, keepdims=True)
    scale_inv = lax.rsqrt(total / depth + epsilon)
    for start in range(0, depth, step):
        values = tokens[start : start + step].astype(jnp.float32)
        normed[start : start + step] = (values * scale_inv).astype(jnp.bfloat16)


def begin(tokens):
    return kernel_call(begin_kernel, like(tokens.shape), tokens, scalars=0)


def relay_kernel(place, beside, across, out):
    core = place[1] % 2
    for k, block in enumerate((across, beside)):

        @pl.when(core == k)
        def _():
            out[...] = block[...]


def relay(place, beside, across):
    return kernel_call(relay_kernel, like(beside.shape), place, beside, across)


def spaced(rows):
    gap = -rows.shape[0] % 16
    return jnp.concatenate([rows, jnp.zeros((gap, rows.shape[1]), rows.dtype)], axis=0)


def room_of(rows):
    return (rows + 15) // 16 * 16


def weights_kernel(w_keyval, w_query, out):
    out[: w_keyval.shape[0]] = w_keyval[...]
    out[w_keyval.shape[0] :] = w_query[...]


def weights_of(w_keyval, w_query):
    rows, depth = w_keyval.shape[0] + w_query.shape[0], w_query.shape[1]
    return kernel_call(weights_kernel, like((rows, depth)), w_keyval, w_query, scalars=0)


def last_kernel(place, inner, outer, out):
    z = place[0]
    middle = (z == 1) | (z == 2)
    for flag, rows in ((middle, inner), (jnp.logical_not(middle), outer)):

        @pl.when(flag)
        def _():
            out[...] = rows[...]


def last_of(place, inner, outer):
    return kernel_call(last_kernel, like(inner.shape), place, inner, outer)


def add_states(z, totals, lin):
    keys_first = z < 2
    tokens = lin.shape[1]
    ones = (lax.broadcasted_iota(jnp.int32, (16, tokens), 0) == 0).astype(jnp.bfloat16)
    one, two = lin[:HDIM], lin[HDIM:]
    key = jnp.maximum(jnp.where(keys_first, one, two), 0.0).astype(jnp.bfloat16)
    value = jnp.where(keys_first, two, one).astype(jnp.bfloat16)
    return totals + lax.dot_general(
        jnp.concatenate([value, ones], axis=0),
        key,
        (((1,), (1,)), ((), ())),
        preferred_element_type=jnp.float32,
    )


def ready_kernel(*refs):
    *blocks, keyval, keyval_there, query = refs
    own, first, second = range(3)
    room = query.shape[0] // 6
    for i, out in enumerate((keyval, keyval_there)):
        rows = blocks[3 * i : 3 * i + 3]
        for k, one in enumerate((first, own, second)):
            out[HDIM * k : HDIM * (k + 1)] = rows[one][:HDIM]
        for k in range(3):
            at = (3 * i + k) * room
            query[at : at + room] = spaced(rows[k][HDIM:])


def ready_rows(mine, there):
    rows, depth = mine[0].shape
    outs = (like((3 * HDIM, depth)),) * 2 + (like((6 * room_of(rows - HDIM), depth)),)
    return kernel_call(ready_kernel, outs, *mine, *there, scalars=0)


def state_kernel(place, mine, there, *refs):
    *blocks, out = refs
    for i, rows in enumerate((mine, there)):
        total = 0.0
        for block in blocks:
            lin = jnp.dot(rows[HDIM:], block[...], preferred_element_type=jnp.float32)
            total = add_states(place[0], total, lin)
        out[i] = total


def states_of(place, mine, there, blocks):
    depth, tokens = blocks[0].shape
    return kernel_call(
        state_kernel,
        like((2, HDIM + 16, HDIM), jnp.float32),
        place,
        mine,
        there,
        *blocks,
        flops=8 * HDIM * depth * len(blocks) * tokens,
    )


def late_kernel(core, place, part, rows, last, *refs):
    *blocks, out, held, keys, values = refs
    z = place[0]
    odd, keys_first = z % 2 == 1, z < 2
    held[:HDIM] = rows[:HDIM]
    held[HDIM:] = last[:HDIM]
    tokens = blocks[0].shape[1]
    ones = (lax.broadcasted_iota(jnp.int32, (16, tokens), 0) == 0).astype(jnp.bfloat16)
    for k, block in enumerate(blocks):
        lin = jnp.dot(held[...], block[...], preferred_element_type=jnp.float32)
        to = slice(tokens * k, tokens * (k + 1))
        one, two = lin[:HDIM], lin[HDIM:]
        key = jnp.maximum(jnp.where(keys_first, one, two), 0.0)
        keys[:, to] = key.astype(jnp.bfloat16)
        values[:HDIM, to] = jnp.where(keys_first, two, one).astype(jnp.bfloat16)
        values[HDIM:, to] = ones
    total = lax.dot_general(
        values[...], keys[...], (((1,), (1,)), ((), ())), preferred_element_type=jnp.float32
    )
    out[0] = jnp.where(odd, total, part[core])
    out[1] = jnp.where(odd, part[core], total)


def late_states(core, place, part, rows, last, blocks):
    depth, tokens = blocks[0].shape
    columns = len(blocks) * tokens
    return kernel_call(
        functools.partial(late_kernel, core),
        like(part.shape, part.dtype),
        place,
        part,
        rows,
        last,
        *blocks,
        scratch=[
            pltpu.VMEM((2 * HDIM, depth), jnp.bfloat16),
            pltpu.VMEM((HDIM, columns), jnp.bfloat16),
            pltpu.VMEM((HDIM + 16, columns), jnp.bfloat16),
        ],
        flops=4 * HDIM * depth * columns,
    )


def sum_kernel(*refs):
    total = refs[0][...].astype(jnp.float32)
    for one in refs[1:-1]:
        total += one[...].astype(jnp.float32)
    refs[-1][...] = total.astype(refs[-1].dtype)


def sum_of(parts, dtype):
    return kernel_call(sum_kernel, like(parts[0].shape, dtype), *parts, scalars=0)


def query_heads(place, lin, first, one, two, out, columns):
    half = HDIM // 2
    one, two = lin[one : one + half], lin[two : two + half]
    turned = place[1] % 2 == 1
    head = [jnp.where(turned, two, one), jnp.where(turned, one, two)]
    head = jnp.concatenate(head, axis=0)
    rows = pl.ds(pl.multiple_of((place[0] ^ first) * HDIM, 16), HDIM)
    out[rows, columns] = jnp.maximum(head, 0.0).astype(jnp.bfloat16)


def near_query_kernel(place, rows, *refs):
    *blocks, out = refs
    step = rows.shape[0] // 6
    tokens = blocks[0].shape[1]
    for k, block in enumerate(blocks):
        lin = jnp.dot(rows[...], block[...], preferred_element_type=jnp.float32)
        for i in range(3):
            columns = slice(tokens * k, tokens * (k + 1))
            query_heads(place, lin, i, step * i, step * (3 + i), out, columns)


def near_queries(place, rows, blocks):
    tokens = blocks[0].shape[1]
    return kernel_call(
        near_query_kernel, like((LAYERS * HDIM, len(blocks) * tokens)), place, rows, *blocks
    )


def query_kernel(place, near, last, last_there, block_0, block_1, out, held):
    step = held.shape[0] // 2
    held[:step] = spaced(last[HDIM:])
    held[step:] = spaced(last_there[HDIM:])
    out[...] = near[...]
    tokens = block_0.shape[1]
    for k, block in enumerate((block_0, block_1)):
        lin = jnp.dot(held[...], block[...], preferred_element_type=jnp.float32)
        columns = slice(tokens * k, tokens * (k + 1))
        query_heads(place, lin, 3, 0, step, out, columns)


def queries_of(place, near, rows, blocks):
    depth = blocks[0].shape[0]
    return kernel_call(
        query_kernel,
        like(near.shape),
        place,
        near,
        *rows,
        *blocks,
        scratch=[pltpu.VMEM((2 * room_of(HDIM // 2), depth), jnp.bfloat16)],
    )


def attend_kernel(row, strip, place, mine, there, taps, center, side, halo, out):
    z, slot = place[0], place[1]
    y, core = slot // 4, slot % 2
    tokens = out.shape[1]
    columns = slice(tokens * strip, tokens * (strip + 1))
    halo_later = y == row
    halo_there = jnp.where(halo_later, z < LAYERS - 1, z > 0)
    for m in range(LAYERS):
        own, other = mine[m // 2], there[m // 2]
        state = jnp.where(core == m % 2, own, other).astype(jnp.bfloat16)
        rows = pl.ds(HDIM * m, HDIM)

        def attended(frame):
            sums = jnp.dot(state, frame[rows, columns], preferred_element_type=jnp.float32)
            result = sums[:HDIM] * (1.0 / (sums[HDIM : HDIM + 1] + epsilon))
            return result.astype(jnp.bfloat16).astype(jnp.float32)

        tap = taps[rows]
        tap_side = jnp.where(halo_later, tap[:, 0:1], tap[:, 2:3])
        tap_halo = jnp.where(halo_later, tap[:, 2:3], tap[:, 0:1])
        mixed = tap_side * attended(side) + tap[:, 1:2] * attended(center)
        mixed += tap_halo * jnp.where(halo_there, attended(halo), 0.0)
        out[rows] = mixed.astype(jnp.bfloat16)


def attend(row, strip, place, mine, there, taps, *frames):
    channels, tokens = frames[0].shape
    body = functools.partial(attend_kernel, row, strip)
    return kernel_call(
        body, like((channels, tokens // 2)), place, mine, there, taps, *frames
    )


def finish_kernel(place, *refs):
    parts, (out, held) = refs[:4], refs[4:]
    chip = place[1] // 2
    tokens = out.shape[0]
    for k, part in enumerate(parts):
        for m in range(LAYERS):
            to = pl.multiple_of((4 * m + (chip ^ k)) * HDIM, 16)
            held[pl.ds(to, HDIM)] = part[pl.ds(HDIM * m, HDIM)]
    row = lax.broadcasted_iota(jnp.int32, (tokens, tokens), 0)
    column = lax.broadcasted_iota(jnp.int32, (tokens, tokens), 1)
    same = (row == column).astype(jnp.bfloat16)
    step = 256
    for at in range(0, out.shape[1], step):
        out[:, at : at + step] = lax.dot_general(
            same, held[at : at + step], (((1,), (1,)), ((), ())), preferred_element_type=jnp.float32
        ).astype(jnp.bfloat16)


def finish(place, parts):
    channels, tokens = parts[0].shape
    return kernel_call(
        finish_kernel,
        like((tokens, 4 * channels)),
        place,
        *parts,
        scratch=[pltpu.VMEM((4 * channels, tokens), jnp.bfloat16)],
    )


STATE_SENT = jnp.bfloat16
LAYERS = 4
PLANE = 8


def send(value, place):
    pairs = []
    for z in range(LAYERS):
        for slot in range(PLANE):
            to = place(z, slot)
            if to is not None:
                pairs.append((z * PLANE + slot, to[0] * PLANE + to[1]))
    return lax.ppermute(value, "frame", pairs)


def swap(value, bits):
    return send(value, lambda z, slot: (z, slot ^ bits))


def between(value, steps):
    return send(value, lambda z, slot: (steps[z], slot) if z in steps else None)


def together(*values):
    return lax.optimization_barrier(values)


def planes(tokens, w_query, w_keyval, taps):
    me = lax.axis_index("frame")
    z, slot = me // PLANE, me % PLANE
    chip = slot // 2
    place = jnp.stack([z, slot]).astype(jnp.int32)

    cross = [{i: i ^ k for i in range(LAYERS)} for k in range(LAYERS)]
    inner, outer = {1: 2, 2: 1}, {1: 0, 2: 3}

    by_head = taps.reshape(3, LAYERS, 4, HDIM)
    tap = lax.dynamic_index_in_dim(by_head, chip, axis=2, keepdims=False).reshape(3, -1).T
    weights = weights_of(w_keyval, w_query)
    weights_2 = between(weights, cross[2])
    weights_1 = between(weights, cross[1])
    own = begin(tokens.T)
    beside, across = swap(own, 2), swap(own, 4)
    weights_there = swap(weights, 1)
    weights_2, weights_1, weights, own, beside, across, weights_there, tap = together(
        weights_2, weights_1, weights, own, beside, across, weights_there, tap
    )

    weights_inner = between(weights, inner)
    weights_outer = between(weights_2, outer)
    passed = relay(place, beside, across)
    diagonal = send(passed, lambda z, slot: (z, slot ^ (4 if slot % 2 else 2)))
    there_2, there_1 = swap(weights_2, 1), swap(weights_1, 1)
    keyval, keyval_there, query = ready_rows(
        (weights, weights_1, weights_2), (weights_there, there_1, there_2)
    )
    blocks = (own, beside, across, diagonal)
    part = states_of(place, keyval, keyval_there, blocks)
    near_here = near_queries(place, query, (own, beside))
    near_there = near_queries(place, query, (across, diagonal))
    diagonal, weights_inner, weights_outer, part, near_here, near_there = together(
        diagonal, weights_inner, weights_outer, part, near_here, near_there
    )

    weights_3 = last_of(place, weights_inner, weights_outer)
    there_3 = swap(weights_3, 1)
    kept = late_states(0, place, part, keyval, weights_3, blocks)
    given = late_states(1, place, part, keyval_there, there_3, blocks)
    kept, given, near_here = together(kept, given, near_here)
    rows = (weights_3, there_3)
    here = queries_of(place, near_here, rows, (own, beside))
    there = queries_of(place, near_there, rows, (across, diagonal))
    kept, here = together(kept, here)
    part = sum_of([kept, swap(given, 1)], STATE_SENT)
    parts = [part] + [between(part, cross[k]) for k in (2, 3, 1)]
    here, parts[3] = together(here, parts[3])
    there, *parts = together(there, *parts)
    state = sum_of(parts, STATE_SENT)
    state, state_there = (
        send(state, lambda z, slot, flip=flip: (z, 2 * (slot % 4) + (slot // 4 ^ flip)))
        for flip in range(2)
    )

    def aside(value, row):
        def to(z, slot):
            z += 1 if slot // 4 == row else -1
            return (z, slot) if 0 <= z < LAYERS else None

        return send(value, to)


    halo_there, halo_here = aside(here, 1), aside(there, 0)
    states = (state, state_there, tap)
    got_across = [
        swap(attend(0, strip, place, *states, there, here, halo_there), 4 + 2 * strip)
        for strip in range(2)
    ]
    got_beside = swap(attend(1, 1, place, *states, here, there, halo_here), 2)
    kept_here = attend(1, 0, place, *states, here, there, halo_here)
    return finish(place, [kept_here, got_beside, *got_across])


def local(tokens, w_query, w_keyval, taps):
    fits = (
        lax.axis_size("frame") == LAYERS * PLANE
        and HEADS == 2 * PLANE
        and w_keyval.shape[0] == HDIM
        and 2 * w_query.shape[0] == HDIM
        and PLANE * tokens.shape[0] == 2 * HEIGHT * WIDTH
    )
    return (planes if fits else gathered)(tokens, w_query, w_keyval, taps)


def solution(mesh):
    placed = (P(("grp", "frame"), None), P("frame", None), P("frame", None), P())
    return jax.shard_map(
        local, mesh=mesh, in_specs=placed, out_specs=P(("grp", "frame"), None), check_vma=False
    )
```

```python
import functools

import jax
import jax.numpy as jnp
from jax import lax
from jax.experimental import pallas as pl
from jax.experimental.pallas import tpu as pltpu
from jax.sharding import PartitionSpec as P

HEADS = 16
HDIM = 112
HEIGHT = 32
WIDTH = 32


epsilon = 1e-06


def from_behind(value, axis, steps):
    count = lax.axis_size(axis)
    leading, last = (max(0, -steps), min(count, count - steps))
    return lax.ppermute(value, axis, [(source, source + steps) for source in range(leading, last)])


def normalize(rows_in):
    values = rows_in.astype(jnp.float32)
    scale_inv = lax.rsqrt(jnp.mean(values * values, axis=-1, keepdims=True) + epsilon)
    return (values * scale_inv).astype(jnp.bfloat16)


def gathered(tokens, w_query, w_keyval, taps):
    channels = HEADS * HDIM
    rows_here = tokens.shape[0]
    normed = normalize(tokens)

    def project_rows(weight_rows):
        return lax.dot_general(
            normed, weight_rows, (((1,), (1,)), ((), ())), preferred_element_type=jnp.float32
        )

    keyval_lin = project_rows(lax.all_gather(w_keyval, "frame", axis=0, tiled=True))
    key_feats = jax.nn.relu(keyval_lin[:, :channels]).astype(jnp.bfloat16)
    value_proj = keyval_lin[:, channels:].astype(jnp.bfloat16)
    key_heads = key_feats.reshape(rows_here, HEADS, HDIM)
    value_heads = value_proj.reshape(rows_here, HEADS, HDIM)
    local_state = jnp.einsum(
        "thd,the->hde", key_heads, value_heads, preferred_element_type=jnp.float32
    )
    local_keys = jnp.sum(key_heads.astype(jnp.float32), axis=0)
    query_lin = project_rows(lax.all_gather(w_query, "frame", axis=0, tiled=True))
    query_feats = jax.nn.relu(query_lin).astype(jnp.bfloat16)
    state, key_total = lax.psum((local_state, local_keys), "frame")
    query_heads = query_feats.reshape(rows_here, HEADS, HDIM).astype(jnp.float32)
    numer = jnp.einsum("thd,hde->the", query_heads, state, precision=lax.Precision.HIGHEST)
    denom = (
        jnp.einsum("thd,hd->th", query_heads, key_total, precision=lax.Precision.HIGHEST) + epsilon
    )
    attended = (numer / denom[:, :, None]).reshape(rows_here, channels).astype(jnp.bfloat16)
    strips = HEIGHT * WIDTH // rows_here
    earlier = from_behind(attended, "frame", strips)
    later_frame = from_behind(attended, "frame", -strips)
    mixed = (
        taps[0] * earlier.astype(jnp.float32)
        + taps[1] * attended.astype(jnp.float32)
        + taps[2] * later_frame.astype(jnp.float32)
    ).astype(jnp.bfloat16)
    return mixed


VMEM = pl.BlockSpec(memory_space=pltpu.VMEM)
SMEM = pl.BlockSpec(memory_space=pltpu.SMEM)
ANY = pl.BlockSpec(memory_space=pl.ANY)
PARAMS = pltpu.CompilerParams(vmem_limit_bytes=16 * 2**20)


def kernel_call(body, outs, *operands, scalars=1, scratch=(), flops=0):
    moved = sum(one.size * one.dtype.itemsize for one in operands)
    return pl.pallas_call(
        body,
        out_shape=outs,
        in_specs=[SMEM] * scalars + [VMEM] * (len(operands) - scalars),
        out_specs=jax.tree.map(lambda _: VMEM, outs),
        scratch_shapes=list(scratch),
        compiler_params=PARAMS,
        cost_estimate=pl.CostEstimate(flops=flops, bytes_accessed=moved, transcendentals=0),
    )(*operands)


def like(shape, dtype=jnp.bfloat16):
    return jax.ShapeDtypeStruct(shape, dtype)


def begin_kernel(tokens, low, high):
    depth = tokens.shape[0]
    step = depth // 10
    total = jnp.zeros((1, tokens.shape[1]), jnp.float32)
    for start in range(0, depth, step):
        values = tokens[start : start + step].astype(jnp.float32)
        total += jnp.sum(values * values, axis=0, keepdims=True)
    scale_inv = lax.rsqrt(total / depth + epsilon)
    for start in range(0, depth, step):
        values = tokens[start : start + step].astype(jnp.float32)
        half, at = (low, start) if start < depth // 2 else (high, start - depth // 2)
        half[at : at + step] = (values * scale_inv).astype(jnp.bfloat16)


def begin(tokens):
    depth, count = tokens.shape
    outs = (like((depth // 2, count)),) * 2
    return kernel_call(begin_kernel, outs, tokens, scalars=0)


def relay_kernel(place, *refs):
    *halves, out = refs
    core = place[1] % 2
    depth = halves[0].shape[0]
    for k, block in enumerate((halves[2:], halves[:2])):

        @pl.when(core == k)
        def _():
            out[:depth] = block[0][...]
            out[depth:] = block[1][...]


def relay(place, beside, across):
    depth, count = beside[0].shape
    return kernel_call(relay_kernel, like((2 * depth, count)), place, *beside, *across)


def whole_kernel(low, high, out):
    depth = low.shape[0]
    out[:depth] = low[...]
    out[depth:] = high[...]


def whole(halves):
    depth, count = halves[0].shape
    return kernel_call(whole_kernel, like((2 * depth, count)), *halves, scalars=0)


def spaced(rows):
    gap = -rows.shape[0] % 16
    return jnp.concatenate([rows, jnp.zeros((gap, rows.shape[1]), rows.dtype)], axis=0)


def room_of(rows):
    return (rows + 15) // 16 * 16


def weights_kernel(w_keyval, w_query, out):
    out[: w_keyval.shape[0]] = w_keyval[...]
    out[w_keyval.shape[0] :] = w_query[...]


def weights_of(w_keyval, w_query):
    rows, depth = w_keyval.shape[0] + w_query.shape[0], w_query.shape[1]
    return kernel_call(weights_kernel, like((rows, depth)), w_keyval, w_query, scalars=0)


def last_kernel(place, inner, outer, out):
    z = place[0]
    middle = (z == 1) | (z == 2)
    for flag, rows in ((middle, inner), (jnp.logical_not(middle), outer)):

        @pl.when(flag)
        def _():
            out[...] = rows[...]


def last_of(place, inner, outer):
    return kernel_call(last_kernel, like(inner.shape), place, inner, outer)


def add_states(z, totals, lin):
    keys_first = z < 2
    tokens = lin.shape[1]
    ones = (lax.broadcasted_iota(jnp.int32, (16, tokens), 0) == 0).astype(jnp.bfloat16)
    one, two = lin[:HDIM], lin[HDIM:]
    key = jnp.maximum(jnp.where(keys_first, one, two), 0.0).astype(jnp.bfloat16)
    value = jnp.where(keys_first, two, one).astype(jnp.bfloat16)
    return totals + lax.dot_general(
        jnp.concatenate([value, ones], axis=0),
        key,
        (((1,), (1,)), ((), ())),
        preferred_element_type=jnp.float32,
    )


def ready_kernel(*refs):
    *blocks, keyval, keyval_there, query = refs
    own, first, second = range(3)
    room = query.shape[0] // 6
    for i, out in enumerate((keyval, keyval_there)):
        rows = blocks[3 * i : 3 * i + 3]
        for k, one in enumerate((first, own, second)):
            out[HDIM * k : HDIM * (k + 1)] = rows[one][:HDIM]
        for k in range(3):
            at = (3 * i + k) * room
            query[at : at + room] = spaced(rows[k][HDIM:])


def ready_rows(mine, there):
    rows, depth = mine[0].shape
    outs = (like((3 * HDIM, depth)),) * 2 + (like((6 * room_of(rows - HDIM), depth)),)
    return kernel_call(ready_kernel, outs, *mine, *there, scalars=0)


def state_kernel(place, mine, there, *refs):
    *blocks, out = refs
    for i, rows in enumerate((mine, there)):
        total = 0.0
        for block in blocks:
            lin = jnp.dot(rows[HDIM:], block[...], preferred_element_type=jnp.float32)
            total = add_states(place[0], total, lin)
        out[i] = total


def states_of(place, mine, there, blocks):
    depth, tokens = blocks[0].shape
    return kernel_call(
        state_kernel,
        like((2, HDIM + 16, HDIM), jnp.float32),
        place,
        mine,
        there,
        *blocks,
        flops=8 * HDIM * depth * len(blocks) * tokens,
    )


def late_kernel(core, place, part, rows, last, *refs):
    *blocks, out, held, keys, values = refs
    z = place[0]
    odd, keys_first = z % 2 == 1, z < 2
    held[:HDIM] = rows[:HDIM]
    held[HDIM:] = last[:HDIM]
    tokens = blocks[0].shape[1]
    ones = (lax.broadcasted_iota(jnp.int32, (16, tokens), 0) == 0).astype(jnp.bfloat16)
    for k, block in enumerate(blocks):
        lin = jnp.dot(held[...], block[...], preferred_element_type=jnp.float32)
        to = slice(tokens * k, tokens * (k + 1))
        one, two = lin[:HDIM], lin[HDIM:]
        key = jnp.maximum(jnp.where(keys_first, one, two), 0.0)
        keys[:, to] = key.astype(jnp.bfloat16)
        values[:HDIM, to] = jnp.where(keys_first, two, one).astype(jnp.bfloat16)
        values[HDIM:, to] = ones
    total = lax.dot_general(
        values[...], keys[...], (((1,), (1,)), ((), ())), preferred_element_type=jnp.float32
    )
    out[0] = jnp.where(odd, total, part[core])
    out[1] = jnp.where(odd, part[core], total)


def late_states(core, place, part, rows, last, blocks):
    depth, tokens = blocks[0].shape
    columns = len(blocks) * tokens
    return kernel_call(
        functools.partial(late_kernel, core),
        like(part.shape, part.dtype),
        place,
        part,
        rows,
        last,
        *blocks,
        scratch=[
            pltpu.VMEM((2 * HDIM, depth), jnp.bfloat16),
            pltpu.VMEM((HDIM, columns), jnp.bfloat16),
            pltpu.VMEM((HDIM + 16, columns), jnp.bfloat16),
        ],
        flops=4 * HDIM * depth * columns,
    )


def sum_kernel(*refs):
    total = refs[0][...].astype(jnp.float32)
    for one in refs[1:-1]:
        total += one[...].astype(jnp.float32)
    refs[-1][...] = total.astype(refs[-1].dtype)


def sum_of(parts, dtype):
    return kernel_call(sum_kernel, like(parts[0].shape, dtype), *parts, scalars=0)


def query_heads(place, lin, first, one, two, out, columns):
    half = HDIM // 2
    one, two = lin[one : one + half], lin[two : two + half]
    turned = place[1] % 2 == 1
    head = [jnp.where(turned, two, one), jnp.where(turned, one, two)]
    head = jnp.concatenate(head, axis=0)
    rows = pl.ds(pl.multiple_of((place[0] ^ first) * HDIM, 16), HDIM)
    out[rows, columns] = jnp.maximum(head, 0.0).astype(jnp.bfloat16)


def near_query_kernel(place, rows, *refs):
    *blocks, out = refs
    step = rows.shape[0] // 6
    tokens = blocks[0].shape[1]
    for k, block in enumerate(blocks):
        lin = jnp.dot(rows[...], block[...], preferred_element_type=jnp.float32)
        for i in range(3):
            columns = slice(tokens * k, tokens * (k + 1))
            query_heads(place, lin, i, step * i, step * (3 + i), out, columns)


def near_queries(place, rows, blocks):
    tokens = blocks[0].shape[1]
    return kernel_call(
        near_query_kernel, like((LAYERS * HDIM, len(blocks) * tokens)), place, rows, *blocks
    )


def query_kernel(place, near, last, last_there, block_0, block_1, out, held):
    step = held.shape[0] // 2
    held[:step] = spaced(last[HDIM:])
    held[step:] = spaced(last_there[HDIM:])
    out[...] = near[...]
    tokens = block_0.shape[1]
    for k, block in enumerate((block_0, block_1)):
        lin = jnp.dot(held[...], block[...], preferred_element_type=jnp.float32)
        columns = slice(tokens * k, tokens * (k + 1))
        query_heads(place, lin, 3, 0, step, out, columns)


def queries_of(place, near, rows, blocks):
    depth = blocks[0].shape[0]
    return kernel_call(
        query_kernel,
        like(near.shape),
        place,
        near,
        *rows,
        *blocks,
        scratch=[pltpu.VMEM((2 * room_of(HDIM // 2), depth), jnp.bfloat16)],
    )


def attend_kernel(row, strip, place, mine, there, taps, center, side, halo, out):
    z, slot = place[0], place[1]
    y, core = slot // 4, slot % 2
    tokens = out.shape[1]
    columns = slice(tokens * strip, tokens * (strip + 1))
    halo_later = y == row
    halo_there = jnp.where(halo_later, z < LAYERS - 1, z > 0)
    for m in range(LAYERS):
        own, other = mine[m // 2], there[m // 2]
        state = jnp.where(core == m % 2, own, other).astype(jnp.bfloat16)
        rows = pl.ds(HDIM * m, HDIM)

        def attended(frame):
            sums = jnp.dot(state, frame[rows, columns], preferred_element_type=jnp.float32)
            result = sums[:HDIM] * (1.0 / (sums[HDIM : HDIM + 1] + epsilon))
            return result.astype(jnp.bfloat16).astype(jnp.float32)

        tap = taps[rows]
        tap_side = jnp.where(halo_later, tap[:, 0:1], tap[:, 2:3])
        tap_halo = jnp.where(halo_later, tap[:, 2:3], tap[:, 0:1])
        mixed = tap_side * attended(side) + tap[:, 1:2] * attended(center)
        mixed += tap_halo * jnp.where(halo_there, attended(halo), 0.0)
        out[rows] = mixed.astype(jnp.bfloat16)


def attend(row, strip, place, mine, there, taps, *frames):
    channels, tokens = frames[0].shape
    body = functools.partial(attend_kernel, row, strip)
    return kernel_call(
        body, like((channels, tokens // 2)), place, mine, there, taps, *frames
    )


def finish_kernel(place, *refs):
    parts, (out, held) = refs[:4], refs[4:]
    chip = place[1] // 2
    tokens = out.shape[0]
    for k, part in enumerate(parts):
        for m in range(LAYERS):
            to = pl.multiple_of((4 * m + (chip ^ k)) * HDIM, 16)
            held[pl.ds(to, HDIM)] = part[pl.ds(HDIM * m, HDIM)]
    row = lax.broadcasted_iota(jnp.int32, (tokens, tokens), 0)
    column = lax.broadcasted_iota(jnp.int32, (tokens, tokens), 1)
    same = (row == column).astype(jnp.bfloat16)
    step = 256
    for at in range(0, out.shape[1], step):
        out[:, at : at + step] = lax.dot_general(
            same, held[at : at + step], (((1,), (1,)), ((), ())), preferred_element_type=jnp.float32
        ).astype(jnp.bfloat16)


def finish(place, parts):
    channels, tokens = parts[0].shape
    return kernel_call(
        finish_kernel,
        like((tokens, 4 * channels)),
        place,
        *parts,
        scratch=[pltpu.VMEM((4 * channels, tokens), jnp.bfloat16)],
    )


STATE_SENT = jnp.bfloat16
LAYERS = 4
PLANE = 8


def send(value, place):
    pairs = []
    for z in range(LAYERS):
        for slot in range(PLANE):
            to = place(z, slot)
            if to is not None:
                pairs.append((z * PLANE + slot, to[0] * PLANE + to[1]))
    return lax.ppermute(value, "frame", pairs)


def swap(value, bits):
    return send(value, lambda z, slot: (z, slot ^ bits))


def between(value, steps):
    return send(value, lambda z, slot: (steps[z], slot) if z in steps else None)


def together(*values):
    return lax.optimization_barrier(values)


def planes(tokens, w_query, w_keyval, taps):
    me = lax.axis_index("frame")
    z, slot = me // PLANE, me % PLANE
    chip = slot // 2
    place = jnp.stack([z, slot]).astype(jnp.int32)

    cross = [{i: i ^ k for i in range(LAYERS)} for k in range(LAYERS)]
    inner, outer = {1: 2, 2: 1}, {1: 0, 2: 3}

    by_head = taps.reshape(3, LAYERS, 4, HDIM)
    tap = lax.dynamic_index_in_dim(by_head, chip, axis=2, keepdims=False).reshape(3, -1).T
    weights = weights_of(w_keyval, w_query)
    weights_2 = between(weights, cross[2])
    weights_1 = between(weights, cross[1])
    own = begin(tokens.T)
    beside, across = ([swap(half, bits) for half in own] for bits in (2, 4))
    weights_2, weights_1, weights, *halves, tap = together(
        weights_2, weights_1, weights, *own, *beside, *across, tap
    )
    own, beside, across = halves[:2], halves[2:4], halves[4:]
    weights_there = swap(weights, 1)

    weights_inner = between(weights, inner)
    weights_outer = between(weights_2, outer)
    passed = relay(place, beside, across)
    diagonal = send(passed, lambda z, slot: (z, slot ^ (4 if slot % 2 else 2)))
    there_2, there_1 = swap(weights_2, 1), swap(weights_1, 1)
    own, beside, across = whole(own), whole(beside), whole(across)
    keyval, keyval_there, query = ready_rows(
        (weights, weights_1, weights_2), (weights_there, there_1, there_2)
    )
    blocks = (own, beside, across, diagonal)
    part = states_of(place, keyval, keyval_there, blocks)
    near_here = near_queries(place, query, (own, beside))
    near_there = near_queries(place, query, (across, diagonal))
    diagonal, weights_inner, weights_outer, part, near_here, near_there = together(
        diagonal, weights_inner, weights_outer, part, near_here, near_there
    )

    weights_3 = last_of(place, weights_inner, weights_outer)
    there_3 = swap(weights_3, 1)
    kept = late_states(0, place, part, keyval, weights_3, blocks)
    given = late_states(1, place, part, keyval_there, there_3, blocks)
    kept, given, near_here = together(kept, given, near_here)
    rows = (weights_3, there_3)
    here = queries_of(place, near_here, rows, (own, beside))
    there = queries_of(place, near_there, rows, (across, diagonal))
    kept, here = together(kept, here)
    part = sum_of([kept, swap(given, 1)], STATE_SENT)
    parts = [part] + [between(part, cross[k]) for k in (2, 3, 1)]
    here, parts[3] = together(here, parts[3])
    there, *parts = together(there, *parts)
    state = sum_of(parts, STATE_SENT)
    state, state_there = (
        send(state, lambda z, slot, flip=flip: (z, 2 * (slot % 4) + (slot // 4 ^ flip)))
        for flip in range(2)
    )

    def aside(value, row):
        def to(z, slot):
            z += 1 if slot // 4 == row else -1
            return (z, slot) if 0 <= z < LAYERS else None

        return send(value, to)


    halo_there, halo_here = aside(here, 1), aside(there, 0)
    states = (state, state_there, tap)
    got_across = [
        swap(attend(0, strip, place, *states, there, here, halo_there), 4 + 2 * strip)
        for strip in range(2)
    ]
    got_beside = swap(attend(1, 1, place, *states, here, there, halo_here), 2)
    kept_here = attend(1, 0, place, *states, here, there, halo_here)
    return finish(place, [kept_here, got_beside, *got_across])


def local(tokens, w_query, w_keyval, taps):
    fits = (
        lax.axis_size("frame") == LAYERS * PLANE
        and HEADS == 2 * PLANE
        and w_keyval.shape[0] == HDIM
        and 2 * w_query.shape[0] == HDIM
        and PLANE * tokens.shape[0] == 2 * HEIGHT * WIDTH
    )
    return (planes if fits else gathered)(tokens, w_query, w_keyval, taps)


def solution(mesh):
    placed = (P(("grp", "frame"), None), P("frame", None), P("frame", None), P())
    return jax.shard_map(
        local, mesh=mesh, in_specs=placed, out_specs=P(("grp", "frame"), None), check_vma=False
    )
```

```python
import functools

import jax
import jax.numpy as jnp
from jax import lax
from jax.experimental import pallas as pl
from jax.experimental.pallas import tpu as pltpu
from jax.sharding import PartitionSpec as P

HEADS = 16
HDIM = 112
HEIGHT = 32
WIDTH = 32


epsilon = 1e-06


def from_behind(value, axis, steps):
    count = lax.axis_size(axis)
    leading, last = (max(0, -steps), min(count, count - steps))
    return lax.ppermute(value, axis, [(source, source + steps) for source in range(leading, last)])


def normalize(rows_in):
    values = rows_in.astype(jnp.float32)
    scale_inv = lax.rsqrt(jnp.mean(values * values, axis=-1, keepdims=True) + epsilon)
    return (values * scale_inv).astype(jnp.bfloat16)


def gathered(tokens, w_query, w_keyval, taps):
    channels = HEADS * HDIM
    rows_here = tokens.shape[0]
    normed = normalize(tokens)

    def project_rows(weight_rows):
        return lax.dot_general(
            normed, weight_rows, (((1,), (1,)), ((), ())), preferred_element_type=jnp.float32
        )

    keyval_lin = project_rows(lax.all_gather(w_keyval, "frame", axis=0, tiled=True))
    key_feats = jax.nn.relu(keyval_lin[:, :channels]).astype(jnp.bfloat16)
    value_proj = keyval_lin[:, channels:].astype(jnp.bfloat16)
    key_heads = key_feats.reshape(rows_here, HEADS, HDIM)
    value_heads = value_proj.reshape(rows_here, HEADS, HDIM)
    local_state = jnp.einsum(
        "thd,the->hde", key_heads, value_heads, preferred_element_type=jnp.float32
    )
    local_keys = jnp.sum(key_heads.astype(jnp.float32), axis=0)
    query_lin = project_rows(lax.all_gather(w_query, "frame", axis=0, tiled=True))
    query_feats = jax.nn.relu(query_lin).astype(jnp.bfloat16)
    state, key_total = lax.psum((local_state, local_keys), "frame")
    query_heads = query_feats.reshape(rows_here, HEADS, HDIM).astype(jnp.float32)
    numer = jnp.einsum("thd,hde->the", query_heads, state, precision=lax.Precision.HIGHEST)
    denom = (
        jnp.einsum("thd,hd->th", query_heads, key_total, precision=lax.Precision.HIGHEST) + epsilon
    )
    attended = (numer / denom[:, :, None]).reshape(rows_here, channels).astype(jnp.bfloat16)
    strips = HEIGHT * WIDTH // rows_here
    earlier = from_behind(attended, "frame", strips)
    later_frame = from_behind(attended, "frame", -strips)
    mixed = (
        taps[0] * earlier.astype(jnp.float32)
        + taps[1] * attended.astype(jnp.float32)
        + taps[2] * later_frame.astype(jnp.float32)
    ).astype(jnp.bfloat16)
    return mixed


VMEM = pl.BlockSpec(memory_space=pltpu.VMEM)
SMEM = pl.BlockSpec(memory_space=pltpu.SMEM)
ANY = pl.BlockSpec(memory_space=pl.ANY)
PARAMS = pltpu.CompilerParams(vmem_limit_bytes=16 * 2**20)


def kernel_call(body, outs, *operands, scalars=1, scratch=(), flops=0):
    moved = sum(one.size * one.dtype.itemsize for one in operands)
    return pl.pallas_call(
        body,
        out_shape=outs,
        in_specs=[SMEM] * scalars + [VMEM] * (len(operands) - scalars),
        out_specs=jax.tree.map(lambda _: VMEM, outs),
        scratch_shapes=list(scratch),
        compiler_params=PARAMS,
        cost_estimate=pl.CostEstimate(flops=flops, bytes_accessed=moved, transcendentals=0),
    )(*operands)


def like(shape, dtype=jnp.bfloat16):
    return jax.ShapeDtypeStruct(shape, dtype)


def begin_kernel(tokens, low, high):
    depth = tokens.shape[0]
    step = depth // 10
    total = jnp.zeros((1, tokens.shape[1]), jnp.float32)
    for start in range(0, depth, step):
        values = tokens[start : start + step].astype(jnp.float32)
        total += jnp.sum(values * values, axis=0, keepdims=True)
    scale_inv = lax.rsqrt(total / depth + epsilon)
    for start in range(0, depth, step):
        values = tokens[start : start + step].astype(jnp.float32)
        half, at = (low, start) if start < depth * 2 // 5 else (high, start - depth * 2 // 5)
        half[at : at + step] = (values * scale_inv).astype(jnp.bfloat16)


def begin(tokens):
    depth, count = tokens.shape
    cut = depth * 2 // 5
    return kernel_call(
        begin_kernel, (like((cut, count)), like((depth - cut, count))), tokens, scalars=0
    )


def relay_kernel(place, *refs):
    *halves, out = refs
    core = place[1] % 2
    cut = halves[0].shape[0]
    for k, block in enumerate((halves[2:], halves[:2])):

        @pl.when(core == k)
        def _():
            out[:cut] = block[0][...]
            out[cut:] = block[1][...]


def relay(place, beside, across):
    depth, count = (sum(half.shape[0] for half in beside), beside[0].shape[1])
    return kernel_call(relay_kernel, like((depth, count)), place, *beside, *across)


def whole_kernel(low, high, out):
    depth = low.shape[0]
    out[:depth] = low[...]
    out[depth:] = high[...]


def whole(halves):
    depth, count = (sum(half.shape[0] for half in halves), halves[0].shape[1])
    return kernel_call(whole_kernel, like((depth, count)), *halves, scalars=0)


def spaced(rows):
    gap = -rows.shape[0] % 16
    return jnp.concatenate([rows, jnp.zeros((gap, rows.shape[1]), rows.dtype)], axis=0)


def room_of(rows):
    return (rows + 15) // 16 * 16


def weights_kernel(w_keyval, w_query, out):
    out[: w_keyval.shape[0]] = w_keyval[...]
    out[w_keyval.shape[0] :] = w_query[...]


def weights_of(w_keyval, w_query):
    rows, depth = w_keyval.shape[0] + w_query.shape[0], w_query.shape[1]
    return kernel_call(weights_kernel, like((rows, depth)), w_keyval, w_query, scalars=0)


def last_kernel(place, inner, outer, out):
    z = place[0]
    middle = (z == 1) | (z == 2)
    for flag, rows in ((middle, inner), (jnp.logical_not(middle), outer)):

        @pl.when(flag)
        def _():
            out[...] = rows[...]


def last_of(place, inner, outer):
    return kernel_call(last_kernel, like(inner.shape), place, inner, outer)


def add_states(z, totals, lin):
    keys_first = z < 2
    tokens = lin.shape[1]
    ones = (lax.broadcasted_iota(jnp.int32, (16, tokens), 0) == 0).astype(jnp.bfloat16)
    one, two = lin[:HDIM], lin[HDIM:]
    key = jnp.maximum(jnp.where(keys_first, one, two), 0.0).astype(jnp.bfloat16)
    value = jnp.where(keys_first, two, one).astype(jnp.bfloat16)
    return totals + lax.dot_general(
        jnp.concatenate([value, ones], axis=0),
        key,
        (((1,), (1,)), ((), ())),
        preferred_element_type=jnp.float32,
    )


def ready_kernel(*refs):
    *blocks, keyval, keyval_there, query = refs
    own, first, second = range(3)
    room = query.shape[0] // 6
    for i, out in enumerate((keyval, keyval_there)):
        rows = blocks[3 * i : 3 * i + 3]
        for k, one in enumerate((first, own, second)):
            out[HDIM * k : HDIM * (k + 1)] = rows[one][:HDIM]
        for k in range(3):
            at = (3 * i + k) * room
            query[at : at + room] = spaced(rows[k][HDIM:])


def ready_rows(mine, there):
    rows, depth = mine[0].shape
    outs = (like((3 * HDIM, depth)),) * 2 + (like((6 * room_of(rows - HDIM), depth)),)
    return kernel_call(ready_kernel, outs, *mine, *there, scalars=0)


def state_kernel(place, mine, there, *refs):
    *blocks, out = refs
    for i, rows in enumerate((mine, there)):
        total = 0.0
        for block in blocks:
            lin = jnp.dot(rows[HDIM:], block[...], preferred_element_type=jnp.float32)
            total = add_states(place[0], total, lin)
        out[i] = total


def states_of(place, mine, there, blocks):
    depth, tokens = blocks[0].shape
    return kernel_call(
        state_kernel,
        like((2, HDIM + 16, HDIM), jnp.float32),
        place,
        mine,
        there,
        *blocks,
        flops=8 * HDIM * depth * len(blocks) * tokens,
    )


def late_kernel(core, place, part, rows, last, *refs):
    *blocks, out, held, keys, values = refs
    z = place[0]
    odd, keys_first = z % 2 == 1, z < 2
    held[:HDIM] = rows[:HDIM]
    held[HDIM:] = last[:HDIM]
    tokens = blocks[0].shape[1]
    ones = (lax.broadcasted_iota(jnp.int32, (16, tokens), 0) == 0).astype(jnp.bfloat16)
    for k, block in enumerate(blocks):
        lin = jnp.dot(held[...], block[...], preferred_element_type=jnp.float32)
        to = slice(tokens * k, tokens * (k + 1))
        one, two = lin[:HDIM], lin[HDIM:]
        key = jnp.maximum(jnp.where(keys_first, one, two), 0.0)
        keys[:, to] = key.astype(jnp.bfloat16)
        values[:HDIM, to] = jnp.where(keys_first, two, one).astype(jnp.bfloat16)
        values[HDIM:, to] = ones
    total = lax.dot_general(
        values[...], keys[...], (((1,), (1,)), ((), ())), preferred_element_type=jnp.float32
    )
    out[0] = jnp.where(odd, total, part[core])
    out[1] = jnp.where(odd, part[core], total)


def late_states(core, place, part, rows, last, blocks):
    depth, tokens = blocks[0].shape
    columns = len(blocks) * tokens
    return kernel_call(
        functools.partial(late_kernel, core),
        like(part.shape, part.dtype),
        place,
        part,
        rows,
        last,
        *blocks,
        scratch=[
            pltpu.VMEM((2 * HDIM, depth), jnp.bfloat16),
            pltpu.VMEM((HDIM, columns), jnp.bfloat16),
            pltpu.VMEM((HDIM + 16, columns), jnp.bfloat16),
        ],
        flops=4 * HDIM * depth * columns,
    )


def sum_kernel(*refs):
    total = refs[0][...].astype(jnp.float32)
    for one in refs[1:-1]:
        total += one[...].astype(jnp.float32)
    refs[-1][...] = total.astype(refs[-1].dtype)


def sum_of(parts, dtype):
    return kernel_call(sum_kernel, like(parts[0].shape, dtype), *parts, scalars=0)


def query_heads(place, lin, first, one, two, out, columns):
    half = HDIM // 2
    one, two = lin[one : one + half], lin[two : two + half]
    turned = place[1] % 2 == 1
    head = [jnp.where(turned, two, one), jnp.where(turned, one, two)]
    head = jnp.concatenate(head, axis=0)
    rows = pl.ds(pl.multiple_of((place[0] ^ first) * HDIM, 16), HDIM)
    out[rows, columns] = jnp.maximum(head, 0.0).astype(jnp.bfloat16)


def near_query_kernel(place, rows, *refs):
    *blocks, out = refs
    step = rows.shape[0] // 6
    tokens = blocks[0].shape[1]
    for k, block in enumerate(blocks):
        lin = jnp.dot(rows[...], block[...], preferred_element_type=jnp.float32)
        for i in range(3):
            columns = slice(tokens * k, tokens * (k + 1))
            query_heads(place, lin, i, step * i, step * (3 + i), out, columns)


def near_queries(place, rows, blocks):
    tokens = blocks[0].shape[1]
    return kernel_call(
        near_query_kernel, like((LAYERS * HDIM, len(blocks) * tokens)), place, rows, *blocks
    )


def query_kernel(place, near, last, last_there, block_0, block_1, out, held):
    step = held.shape[0] // 2
    held[:step] = spaced(last[HDIM:])
    held[step:] = spaced(last_there[HDIM:])
    out[...] = near[...]
    tokens = block_0.shape[1]
    for k, block in enumerate((block_0, block_1)):
        lin = jnp.dot(held[...], block[...], preferred_element_type=jnp.float32)
        columns = slice(tokens * k, tokens * (k + 1))
        query_heads(place, lin, 3, 0, step, out, columns)


def queries_of(place, near, rows, blocks):
    depth = blocks[0].shape[0]
    return kernel_call(
        query_kernel,
        like(near.shape),
        place,
        near,
        *rows,
        *blocks,
        scratch=[pltpu.VMEM((2 * room_of(HDIM // 2), depth), jnp.bfloat16)],
    )


def attend_kernel(row, strip, place, mine, there, taps, center, side, halo, out):
    z, slot = place[0], place[1]
    y, core = slot // 4, slot % 2
    tokens = out.shape[1]
    columns = slice(tokens * strip, tokens * (strip + 1))
    halo_later = y == row
    halo_there = jnp.where(halo_later, z < LAYERS - 1, z > 0)
    for m in range(LAYERS):
        own, other = mine[m // 2], there[m // 2]
        state = jnp.where(core == m % 2, own, other).astype(jnp.bfloat16)
        rows = pl.ds(HDIM * m, HDIM)

        def attended(frame):
            sums = jnp.dot(state, frame[rows, columns], preferred_element_type=jnp.float32)
            result = sums[:HDIM] * (1.0 / (sums[HDIM : HDIM + 1] + epsilon))
            return result.astype(jnp.bfloat16).astype(jnp.float32)

        tap = taps[rows]
        tap_side = jnp.where(halo_later, tap[:, 0:1], tap[:, 2:3])
        tap_halo = jnp.where(halo_later, tap[:, 2:3], tap[:, 0:1])
        mixed = tap_side * attended(side) + tap[:, 1:2] * attended(center)
        mixed += tap_halo * jnp.where(halo_there, attended(halo), 0.0)
        out[rows] = mixed.astype(jnp.bfloat16)


def attend(row, strip, place, mine, there, taps, *frames):
    channels, tokens = frames[0].shape
    body = functools.partial(attend_kernel, row, strip)
    return kernel_call(
        body, like((channels, tokens // 2)), place, mine, there, taps, *frames
    )


def finish_kernel(place, *refs):
    parts, (out, held) = refs[:4], refs[4:]
    chip = place[1] // 2
    tokens = out.shape[0]
    for k, part in enumerate(parts):
        for m in range(LAYERS):
            to = pl.multiple_of((4 * m + (chip ^ k)) * HDIM, 16)
            held[pl.ds(to, HDIM)] = part[pl.ds(HDIM * m, HDIM)]
    row = lax.broadcasted_iota(jnp.int32, (tokens, tokens), 0)
    column = lax.broadcasted_iota(jnp.int32, (tokens, tokens), 1)
    same = (row == column).astype(jnp.bfloat16)
    step = 256
    for at in range(0, out.shape[1], step):
        out[:, at : at + step] = lax.dot_general(
            same, held[at : at + step], (((1,), (1,)), ((), ())), preferred_element_type=jnp.float32
        ).astype(jnp.bfloat16)


def finish(place, parts):
    channels, tokens = parts[0].shape
    return kernel_call(
        finish_kernel,
        like((tokens, 4 * channels)),
        place,
        *parts,
        scratch=[pltpu.VMEM((4 * channels, tokens), jnp.bfloat16)],
    )


STATE_SENT = jnp.bfloat16
LAYERS = 4
PLANE = 8


def send(value, place):
    pairs = []
    for z in range(LAYERS):
        for slot in range(PLANE):
            to = place(z, slot)
            if to is not None:
                pairs.append((z * PLANE + slot, to[0] * PLANE + to[1]))
    return lax.ppermute(value, "frame", pairs)


def swap(value, bits):
    return send(value, lambda z, slot: (z, slot ^ bits))


def between(value, steps):
    return send(value, lambda z, slot: (steps[z], slot) if z in steps else None)


def together(*values):
    return lax.optimization_barrier(values)


def planes(tokens, w_query, w_keyval, taps):
    me = lax.axis_index("frame")
    z, slot = me // PLANE, me % PLANE
    chip = slot // 2
    place = jnp.stack([z, slot]).astype(jnp.int32)

    cross = [{i: i ^ k for i in range(LAYERS)} for k in range(LAYERS)]
    inner, outer = {1: 2, 2: 1}, {1: 0, 2: 3}

    by_head = taps.reshape(3, LAYERS, 4, HDIM)
    tap = lax.dynamic_index_in_dim(by_head, chip, axis=2, keepdims=False).reshape(3, -1).T
    weights = weights_of(w_keyval, w_query)
    weights_2 = between(weights, cross[2])
    weights_1 = between(weights, cross[1])
    own = begin(tokens.T)
    beside, across = ([swap(half, bits) for half in own] for bits in (2, 4))
    weights_2, weights_1, weights, *halves, tap = together(
        weights_2, weights_1, weights, *own, *beside, *across, tap
    )
    own, beside, across = halves[:2], halves[2:4], halves[4:]
    weights_there = swap(weights, 1)

    weights_inner = between(weights, inner)
    weights_outer = between(weights_2, outer)
    passed = relay(place, beside, across)
    diagonal = send(passed, lambda z, slot: (z, slot ^ (4 if slot % 2 else 2)))
    there_2, there_1 = swap(weights_2, 1), swap(weights_1, 1)
    own, beside, across = whole(own), whole(beside), whole(across)
    keyval, keyval_there, query = ready_rows(
        (weights, weights_1, weights_2), (weights_there, there_1, there_2)
    )
    blocks = (own, beside, across, diagonal)
    part = states_of(place, keyval, keyval_there, blocks)
    near_here = near_queries(place, query, (own, beside))
    near_there = near_queries(place, query, (across, diagonal))
    diagonal, weights_inner, weights_outer, part, near_here, near_there = together(
        diagonal, weights_inner, weights_outer, part, near_here, near_there
    )

    weights_3 = last_of(place, weights_inner, weights_outer)
    there_3 = swap(weights_3, 1)
    kept = late_states(0, place, part, keyval, weights_3, blocks)
    given = late_states(1, place, part, keyval_there, there_3, blocks)
    kept, given, near_here = together(kept, given, near_here)
    rows = (weights_3, there_3)
    here = queries_of(place, near_here, rows, (own, beside))
    there = queries_of(place, near_there, rows, (across, diagonal))
    kept, here = together(kept, here)
    part = sum_of([kept, swap(given, 1)], STATE_SENT)
    parts = [part] + [between(part, cross[k]) for k in (2, 3, 1)]
    here, parts[3] = together(here, parts[3])
    there, *parts = together(there, *parts)
    state = sum_of(parts, STATE_SENT)
    state, state_there = (
        send(state, lambda z, slot, flip=flip: (z, 2 * (slot % 4) + (slot // 4 ^ flip)))
        for flip in range(2)
    )

    def aside(value, row):
        def to(z, slot):
            z += 1 if slot // 4 == row else -1
            return (z, slot) if 0 <= z < LAYERS else None

        return send(value, to)


    halo_there, halo_here = aside(here, 1), aside(there, 0)
    states = (state, state_there, tap)
    got_across = [
        swap(attend(0, strip, place, *states, there, here, halo_there), 4 + 2 * strip)
        for strip in range(2)
    ]
    got_beside = swap(attend(1, 1, place, *states, here, there, halo_here), 2)
    kept_here = attend(1, 0, place, *states, here, there, halo_here)
    return finish(place, [kept_here, got_beside, *got_across])


def local(tokens, w_query, w_keyval, taps):
    fits = (
        lax.axis_size("frame") == LAYERS * PLANE
        and HEADS == 2 * PLANE
        and w_keyval.shape[0] == HDIM
        and 2 * w_query.shape[0] == HDIM
        and PLANE * tokens.shape[0] == 2 * HEIGHT * WIDTH
    )
    return (planes if fits else gathered)(tokens, w_query, w_keyval, taps)


def solution(mesh):
    placed = (P(("grp", "frame"), None), P("frame", None), P("frame", None), P())
    return jax.shard_map(
        local, mesh=mesh, in_specs=placed, out_specs=P(("grp", "frame"), None), check_vma=False
    )
```

```python
import functools

import jax
import jax.numpy as jnp
from jax import lax
from jax.experimental import pallas as pl
from jax.experimental.pallas import tpu as pltpu
from jax.sharding import PartitionSpec as P

HEADS = 16
HDIM = 112
HEIGHT = 32
WIDTH = 32


epsilon = 1e-06


def from_behind(value, axis, steps):
    count = lax.axis_size(axis)
    leading, last = (max(0, -steps), min(count, count - steps))
    return lax.ppermute(value, axis, [(source, source + steps) for source in range(leading, last)])


def normalize(rows_in):
    values = rows_in.astype(jnp.float32)
    scale_inv = lax.rsqrt(jnp.mean(values * values, axis=-1, keepdims=True) + epsilon)
    return (values * scale_inv).astype(jnp.bfloat16)


def gathered(tokens, w_query, w_keyval, taps):
    channels = HEADS * HDIM
    rows_here = tokens.shape[0]
    normed = normalize(tokens)

    def project_rows(weight_rows):
        return lax.dot_general(
            normed, weight_rows, (((1,), (1,)), ((), ())), preferred_element_type=jnp.float32
        )

    keyval_lin = project_rows(lax.all_gather(w_keyval, "frame", axis=0, tiled=True))
    key_feats = jax.nn.relu(keyval_lin[:, :channels]).astype(jnp.bfloat16)
    value_proj = keyval_lin[:, channels:].astype(jnp.bfloat16)
    key_heads = key_feats.reshape(rows_here, HEADS, HDIM)
    value_heads = value_proj.reshape(rows_here, HEADS, HDIM)
    local_state = jnp.einsum(
        "thd,the->hde", key_heads, value_heads, preferred_element_type=jnp.float32
    )
    local_keys = jnp.sum(key_heads.astype(jnp.float32), axis=0)
    query_lin = project_rows(lax.all_gather(w_query, "frame", axis=0, tiled=True))
    query_feats = jax.nn.relu(query_lin).astype(jnp.bfloat16)
    state, key_total = lax.psum((local_state, local_keys), "frame")
    query_heads = query_feats.reshape(rows_here, HEADS, HDIM).astype(jnp.float32)
    numer = jnp.einsum("thd,hde->the", query_heads, state, precision=lax.Precision.HIGHEST)
    denom = (
        jnp.einsum("thd,hd->th", query_heads, key_total, precision=lax.Precision.HIGHEST) + epsilon
    )
    attended = (numer / denom[:, :, None]).reshape(rows_here, channels).astype(jnp.bfloat16)
    strips = HEIGHT * WIDTH // rows_here
    earlier = from_behind(attended, "frame", strips)
    later_frame = from_behind(attended, "frame", -strips)
    mixed = (
        taps[0] * earlier.astype(jnp.float32)
        + taps[1] * attended.astype(jnp.float32)
        + taps[2] * later_frame.astype(jnp.float32)
    ).astype(jnp.bfloat16)
    return mixed


VMEM = pl.BlockSpec(memory_space=pltpu.VMEM)
SMEM = pl.BlockSpec(memory_space=pltpu.SMEM)
ANY = pl.BlockSpec(memory_space=pl.ANY)
PARAMS = pltpu.CompilerParams(vmem_limit_bytes=16 * 2**20)


def kernel_call(body, outs, *operands, scalars=1, scratch=(), flops=0):
    moved = sum(one.size * one.dtype.itemsize for one in operands)
    return pl.pallas_call(
        body,
        out_shape=outs,
        in_specs=[SMEM] * scalars + [VMEM] * (len(operands) - scalars),
        out_specs=jax.tree.map(lambda _: VMEM, outs),
        scratch_shapes=list(scratch),
        compiler_params=PARAMS,
        cost_estimate=pl.CostEstimate(flops=flops, bytes_accessed=moved, transcendentals=0),
    )(*operands)


def like(shape, dtype=jnp.bfloat16):
    return jax.ShapeDtypeStruct(shape, dtype)


def begin_kernel(tokens, low, high):
    depth = tokens.shape[0]
    step = depth // 10
    total = jnp.zeros((1, tokens.shape[1]), jnp.float32)
    for start in range(0, depth, step):
        values = tokens[start : start + step].astype(jnp.float32)
        total += jnp.sum(values * values, axis=0, keepdims=True)
    scale_inv = lax.rsqrt(total / depth + epsilon)
    for start in range(0, depth, step):
        values = tokens[start : start + step].astype(jnp.float32)
        half, at = (low, start) if start < depth // 2 else (high, start - depth // 2)
        half[at : at + step] = (values * scale_inv).astype(jnp.bfloat16)


def begin(tokens):
    depth, count = tokens.shape
    outs = (like((depth // 2, count)),) * 2
    return kernel_call(begin_kernel, outs, tokens, scalars=0)


def relay_kernel(place, *refs):
    *halves, out = refs
    core = place[1] % 2
    depth = halves[0].shape[0]
    for k, block in enumerate((halves[2:], halves[:2])):

        @pl.when(core == k)
        def _():
            out[:depth] = block[0][...]
            out[depth:] = block[1][...]


def relay(place, beside, across):
    depth, count = beside[0].shape
    return kernel_call(relay_kernel, like((2 * depth, count)), place, *beside, *across)


def whole_kernel(low, high, out):
    depth = low.shape[0]
    out[:depth] = low[...]
    out[depth:] = high[...]


def whole(halves):
    depth, count = halves[0].shape
    return kernel_call(whole_kernel, like((2 * depth, count)), *halves, scalars=0)


def spaced(rows):
    gap = -rows.shape[0] % 16
    return jnp.concatenate([rows, jnp.zeros((gap, rows.shape[1]), rows.dtype)], axis=0)


def room_of(rows):
    return (rows + 15) // 16 * 16


def weights_kernel(w_keyval, w_query, out):
    out[: w_keyval.shape[0]] = w_keyval[...]
    out[w_keyval.shape[0] :] = w_query[...]


def weights_of(w_keyval, w_query):
    rows, depth = w_keyval.shape[0] + w_query.shape[0], w_query.shape[1]
    return kernel_call(weights_kernel, like((rows, depth)), w_keyval, w_query, scalars=0)


def last_kernel(place, inner, outer, out):
    z = place[0]
    middle = (z == 1) | (z == 2)
    for flag, rows in ((middle, inner), (jnp.logical_not(middle), outer)):

        @pl.when(flag)
        def _():
            out[...] = rows[...]


def last_of(place, inner, outer):
    return kernel_call(last_kernel, like(inner.shape), place, inner, outer)


def add_states(z, totals, lin):
    keys_first = z < 2
    tokens = lin.shape[1]
    ones = (lax.broadcasted_iota(jnp.int32, (16, tokens), 0) == 0).astype(jnp.bfloat16)
    one, two = lin[:HDIM], lin[HDIM:]
    key = jnp.maximum(jnp.where(keys_first, one, two), 0.0).astype(jnp.bfloat16)
    value = jnp.where(keys_first, two, one).astype(jnp.bfloat16)
    return totals + lax.dot_general(
        jnp.concatenate([value, ones], axis=0),
        key,
        (((1,), (1,)), ((), ())),
        preferred_element_type=jnp.float32,
    )


def ready_kernel(*refs):
    *blocks, keyval, keyval_there, query = refs
    own, first, second = range(3)
    room = query.shape[0] // 6
    for i, out in enumerate((keyval, keyval_there)):
        rows = blocks[3 * i : 3 * i + 3]
        for k, one in enumerate((first, own, second)):
            out[HDIM * k : HDIM * (k + 1)] = rows[one][:HDIM]
        for k in range(3):
            at = (3 * i + k) * room
            query[at : at + room] = spaced(rows[k][HDIM:])


def ready_rows(mine, there):
    rows, depth = mine[0].shape
    outs = (like((3 * HDIM, depth)),) * 2 + (like((6 * room_of(rows - HDIM), depth)),)
    return kernel_call(ready_kernel, outs, *mine, *there, scalars=0)


def state_kernel(place, mine, there, *refs):
    *blocks, out = refs
    for i, rows in enumerate((mine, there)):
        total = 0.0
        for block in blocks:
            lin = jnp.dot(rows[HDIM:], block[...], preferred_element_type=jnp.float32)
            total = add_states(place[0], total, lin)
        out[i] = total


def states_of(place, mine, there, blocks):
    depth, tokens = blocks[0].shape
    return kernel_call(
        state_kernel,
        like((2, HDIM + 16, HDIM), jnp.float32),
        place,
        mine,
        there,
        *blocks,
        flops=8 * HDIM * depth * len(blocks) * tokens,
    )


def late_kernel(core, place, part, rows, last, *refs):
    *blocks, out, held, keys, values = refs
    z = place[0]
    odd, keys_first = z % 2 == 1, z < 2
    held[:HDIM] = rows[:HDIM]
    held[HDIM:] = last[:HDIM]
    tokens = blocks[0].shape[1]
    ones = (lax.broadcasted_iota(jnp.int32, (16, tokens), 0) == 0).astype(jnp.bfloat16)
    for k, block in enumerate(blocks):
        lin = jnp.dot(held[...], block[...], preferred_element_type=jnp.float32)
        to = slice(tokens * k, tokens * (k + 1))
        one, two = lin[:HDIM], lin[HDIM:]
        key = jnp.maximum(jnp.where(keys_first, one, two), 0.0)
        keys[:, to] = key.astype(jnp.bfloat16)
        values[:HDIM, to] = jnp.where(keys_first, two, one).astype(jnp.bfloat16)
        values[HDIM:, to] = ones
    total = lax.dot_general(
        values[...], keys[...], (((1,), (1,)), ((), ())), preferred_element_type=jnp.float32
    )
    out[0] = jnp.where(odd, total, part[core])
    out[1] = jnp.where(odd, part[core], total)


def late_states(core, place, part, rows, last, blocks):
    depth, tokens = blocks[0].shape
    columns = len(blocks) * tokens
    return kernel_call(
        functools.partial(late_kernel, core),
        like(part.shape, part.dtype),
        place,
        part,
        rows,
        last,
        *blocks,
        scratch=[
            pltpu.VMEM((2 * HDIM, depth), jnp.bfloat16),
            pltpu.VMEM((HDIM, columns), jnp.bfloat16),
            pltpu.VMEM((HDIM + 16, columns), jnp.bfloat16),
        ],
        flops=4 * HDIM * depth * columns,
    )


def sum_kernel(*refs):
    total = refs[0][...].astype(jnp.float32)
    for one in refs[1:-1]:
        total += one[...].astype(jnp.float32)
    refs[-1][...] = total.astype(refs[-1].dtype)


def sum_of(parts, dtype):
    return kernel_call(sum_kernel, like(parts[0].shape, dtype), *parts, scalars=0)


def query_heads(place, lin, first, one, two, out, columns):
    half = HDIM // 2
    one, two = lin[one : one + half], lin[two : two + half]
    turned = place[1] % 2 == 1
    head = [jnp.where(turned, two, one), jnp.where(turned, one, two)]
    head = jnp.concatenate(head, axis=0)
    rows = pl.ds(pl.multiple_of((place[0] ^ first) * HDIM, 16), HDIM)
    out[rows, columns] = jnp.maximum(head, 0.0).astype(jnp.bfloat16)


def near_query_kernel(place, rows, *refs):
    *blocks, out = refs
    step = rows.shape[0] // 6
    tokens = blocks[0].shape[1]
    for k, block in enumerate(blocks):
        lin = jnp.dot(rows[...], block[...], preferred_element_type=jnp.float32)
        for i in range(3):
            columns = slice(tokens * k, tokens * (k + 1))
            query_heads(place, lin, i, step * i, step * (3 + i), out, columns)


def near_queries(place, rows, blocks):
    tokens = blocks[0].shape[1]
    return kernel_call(
        near_query_kernel, like((LAYERS * HDIM, len(blocks) * tokens)), place, rows, *blocks
    )


def query_kernel(place, near, last, last_there, block_0, block_1, out, held):
    step = held.shape[0] // 2
    held[:step] = spaced(last[HDIM:])
    held[step:] = spaced(last_there[HDIM:])
    out[...] = near[...]
    tokens = block_0.shape[1]
    for k, block in enumerate((block_0, block_1)):
        lin = jnp.dot(held[...], block[...], preferred_element_type=jnp.float32)
        columns = slice(tokens * k, tokens * (k + 1))
        query_heads(place, lin, 3, 0, step, out, columns)


def queries_of(place, near, rows, blocks):
    depth = blocks[0].shape[0]
    return kernel_call(
        query_kernel,
        like(near.shape),
        place,
        near,
        *rows,
        *blocks,
        scratch=[pltpu.VMEM((2 * room_of(HDIM // 2), depth), jnp.bfloat16)],
    )


def attend_kernel(row, strip, place, mine, there, taps, center, side, halo, out):
    z, slot = place[0], place[1]
    y, core = slot // 4, slot % 2
    tokens = out.shape[1]
    columns = slice(tokens * strip, tokens * (strip + 1))
    halo_later = y == row
    halo_there = jnp.where(halo_later, z < LAYERS - 1, z > 0)
    for m in range(LAYERS):
        own, other = mine[m // 2], there[m // 2]
        state = jnp.where(core == m % 2, own, other).astype(jnp.bfloat16)
        rows = pl.ds(HDIM * m, HDIM)

        def attended(frame):
            sums = jnp.dot(state, frame[rows, columns], preferred_element_type=jnp.float32)
            result = sums[:HDIM] * (1.0 / (sums[HDIM : HDIM + 1] + epsilon))
            return result.astype(jnp.bfloat16).astype(jnp.float32)

        tap = taps[rows]
        tap_side = jnp.where(halo_later, tap[:, 0:1], tap[:, 2:3])
        tap_halo = jnp.where(halo_later, tap[:, 2:3], tap[:, 0:1])
        mixed = tap_side * attended(side) + tap[:, 1:2] * attended(center)
        mixed += tap_halo * jnp.where(halo_there, attended(halo), 0.0)
        out[rows] = mixed.astype(jnp.bfloat16)


def attend(row, strip, place, mine, there, taps, *frames):
    channels, tokens = frames[0].shape
    body = functools.partial(attend_kernel, row, strip)
    return kernel_call(
        body, like((channels, tokens // 2)), place, mine, there, taps, *frames
    )


def finish_kernel(place, *refs):
    parts, (out, held) = refs[:4], refs[4:]
    chip = place[1] // 2
    tokens = out.shape[0]
    for k, part in enumerate(parts):
        for m in range(LAYERS):
            to = pl.multiple_of((4 * m + (chip ^ k)) * HDIM, 16)
            held[pl.ds(to, HDIM)] = part[pl.ds(HDIM * m, HDIM)]
    row = lax.broadcasted_iota(jnp.int32, (tokens, tokens), 0)
    column = lax.broadcasted_iota(jnp.int32, (tokens, tokens), 1)
    same = (row == column).astype(jnp.bfloat16)
    step = 256
    for at in range(0, out.shape[1], step):
        out[:, at : at + step] = lax.dot_general(
            same, held[at : at + step], (((1,), (1,)), ((), ())), preferred_element_type=jnp.float32
        ).astype(jnp.bfloat16)


def finish(place, parts):
    channels, tokens = parts[0].shape
    return kernel_call(
        finish_kernel,
        like((tokens, 4 * channels)),
        place,
        *parts,
        scratch=[pltpu.VMEM((4 * channels, tokens), jnp.bfloat16)],
    )


STATE_SENT = jnp.bfloat16
LAYERS = 4
PLANE = 8


def send(value, place):
    pairs = []
    for z in range(LAYERS):
        for slot in range(PLANE):
            to = place(z, slot)
            if to is not None:
                pairs.append((z * PLANE + slot, to[0] * PLANE + to[1]))
    return lax.ppermute(value, "frame", pairs)


def swap(value, bits):
    return send(value, lambda z, slot: (z, slot ^ bits))


def between(value, steps):
    return send(value, lambda z, slot: (steps[z], slot) if z in steps else None)


def together(*values):
    return lax.optimization_barrier(values)


def planes(tokens, w_query, w_keyval, taps):
    me = lax.axis_index("frame")
    z, slot = me // PLANE, me % PLANE
    chip = slot // 2
    place = jnp.stack([z, slot]).astype(jnp.int32)

    cross = [{i: i ^ k for i in range(LAYERS)} for k in range(LAYERS)]
    inner, outer = {1: 2, 2: 1}, {1: 0, 2: 3}

    by_head = taps.reshape(3, LAYERS, 4, HDIM)
    tap = lax.dynamic_index_in_dim(by_head, chip, axis=2, keepdims=False).reshape(3, -1).T
    weights = weights_of(w_keyval, w_query)
    weights_2 = between(weights, cross[2])
    weights_1 = between(weights, cross[1])
    own = begin(tokens.T)
    beside, across = ([swap(half, bits) for half in own] for bits in (2, 4))
    weights_2, weights_1, weights, *halves, tap = together(
        weights_2, weights_1, weights, *own, *beside, *across, tap
    )
    own, beside, across = halves[:2], halves[2:4], halves[4:]
    weights_there = swap(weights, 1)

    weights_inner = between(weights, inner)
    weights_outer = between(weights_2, outer)
    passed = relay(place, beside, across)
    diagonal = send(passed, lambda z, slot: (z, slot ^ (4 if slot % 2 else 2)))
    there_2, there_1 = swap(weights_2, 1), swap(weights_1, 1)
    own, beside, across = whole(own), whole(beside), whole(across)
    keyval, keyval_there, query = ready_rows(
        (weights, weights_1, weights_2), (weights_there, there_1, there_2)
    )
    blocks = (own, beside, across, diagonal)
    part = states_of(place, keyval, keyval_there, blocks)
    near_here = near_queries(place, query, (own, beside))
    near_there = near_queries(place, query, (across, diagonal))
    diagonal, weights_inner, weights_outer, part, near_here, near_there = together(
        diagonal, weights_inner, weights_outer, part, near_here, near_there
    )

    weights_3 = last_of(place, weights_inner, weights_outer)
    there_3 = swap(weights_3, 1)
    kept = late_states(0, place, part, keyval, weights_3, blocks)
    given = late_states(1, place, part, keyval_there, there_3, blocks)
    kept, given, near_here = together(kept, given, near_here)
    rows = (weights_3, there_3)
    here = queries_of(place, near_here, rows, (own, beside))
    there = queries_of(place, near_there, rows, (across, diagonal))
    kept, here = together(kept, here)
    part = sum_of([kept, swap(given, 1)], STATE_SENT)
    parts = [part] + [between(part, cross[k]) for k in (2, 3, 1)]
    here, parts[3] = together(here, parts[3])
    there, *parts = together(there, *parts)
    state = sum_of(parts, STATE_SENT)
    state, state_there = (
        send(state, lambda z, slot, flip=flip: (z, 2 * (slot % 4) + (slot // 4 ^ flip)))
        for flip in range(2)
    )

    def aside(value, row):
        def to(z, slot):
            z += 1 if slot // 4 == row else -1
            return (z, slot) if 0 <= z < LAYERS else None

        return send(value, to)


    halo_there, halo_here = aside(here, 1), aside(there, 0)
    states = (state, state_there, tap)
    corner = attend(0, 1, place, *states, there, here, halo_there)
    got_corner = swap(corner, 6)
    beside_out = attend(1, 1, place, *states, here, there, halo_here)
    across_out = attend(0, 0, place, *states, there, here, halo_there)
    across_out, beside_out = together(across_out, beside_out)
    got_across = [swap(across_out, 4), got_corner]
    got_beside = swap(beside_out, 2)
    kept_here = attend(1, 0, place, *states, here, there, halo_here)
    return finish(place, [kept_here, got_beside, *got_across])


def local(tokens, w_query, w_keyval, taps):
    fits = (
        lax.axis_size("frame") == LAYERS * PLANE
        and HEADS == 2 * PLANE
        and w_keyval.shape[0] == HDIM
        and 2 * w_query.shape[0] == HDIM
        and PLANE * tokens.shape[0] == 2 * HEIGHT * WIDTH
    )
    return (planes if fits else gathered)(tokens, w_query, w_keyval, taps)


def solution(mesh):
    placed = (P(("grp", "frame"), None), P("frame", None), P("frame", None), P())
    return jax.shard_map(
        local, mesh=mesh, in_specs=placed, out_specs=P(("grp", "frame"), None), check_vma=False
    )
```
